1024 devices in a mesh: rep: 128 (over x_lo, z, core), tp: 8 (over y, x_hi).
Axes of the slice: x: 4 (x_hi: 2, x_lo: 2; x = x_hi * 2 + x_lo), y: 4, z: 32, core: 2. Of those that a mesh axis runs over, the one named last changes fastest.
Arguments:
- tokens: bfloat16 [65536, 8192], P(('rep', 'tp')), may hold values from -6 to 6
- base_weight: bfloat16 [8192, 1024], P('tp'), may hold values from -0.0625 to 0.0625
- adapter_down: bfloat16 [128, 8192, 16], P('rep', 'tp'), may hold values from -0.0625 to 0.0625
- adapter_up: bfloat16 [128, 16, 1024], P('rep', None, 'tp'), may hold values from -1.5 to 1.5
- upstream: bfloat16 [65536, 1024], P('rep', 'tp'), may hold values from -3 to 3
- block_tenant_index: int32 [128], replicated, may hold values from 0 to 127
- valid_lengths: int32 [128], replicated, may hold values from 1 to 512, 49152 in all
Outputs:
- projected: bfloat16 [65536, 1024], P('rep', 'tp')
- activation_gradient: bfloat16 [65536, 8192], P('rep', 'tp')
- up_grad: float32 [128, 16, 1024], P('rep', None, 'tp')
The draws below stay inside these ranges and needn't reach their ends.
All inputs are finite; a program needn't handle non-finite values.
Results may differ from the reference program's by a relative error of at most 0.019.
Values may be sent and summed in bfloat16 or wider, within the bound.
No kernel may reach another device: no remote copies, remote signals or barrier semaphores. Data moves between devices by JAX's collectives and lax.ppermute only.
A program may use at most 32 MiB of HBM per device.

```python
import math
import jax
import jax.numpy as jnp
import numpy as np
from jax import lax

MODEL_WIDTH = 8192
VALUE_FEATURES = 1024
R = 16
BLOCK = 512
NBLOCKS = 128
TOKEN_COUNT = 65536
TENANTS = 128
N_TP = 8


def place_ends(array, rng, least, high):
    longest = array.shape.index(max(array.shape))
    spots = []
    for shift in (0, 1):
        where = [jax.random.randint(jax.random.fold_in(rng, axis), (), 0, length) for axis, length in enumerate(array.shape)]
        where[longest] = (where[longest] + shift) % array.shape[longest]
        spots.append(tuple(where))
    return array.at[spots[0]].set(least).at[spots[1]].set(high)


def steps_of(own_key, shape, cuts, low, largest):
    def one(dim, blocks):
        heights = jax.random.uniform(jax.random.fold_in(jax.random.fold_in(own_key, 6), dim), (blocks,), jnp.float32, low / len(cuts), largest / len(cuts))
        return jnp.repeat(jnp.exp(heights), shape[dim] // blocks).reshape((-1,) + (1,) * (len(shape) - dim - 1))

    factor_of = one(*cuts[0])
    for cut in cuts[1:]:
        factor_of = factor_of * one(*cut)
    return factor_of


def rank_table(number_of, slope):
    weights = [(1 << 20) // math.isqrt(standing ** slope) + 1 for standing in range(1, number_of + 1)]
    spread = 1 + sum(weights) // (1 << 30)
    return np.cumsum(np.array([max(1, weight // spread) for weight in weights]))


def ranked_ids(stream_key, shape, amount, lean):
    table = rank_table(amount, lean)
    lot = jax.random.randint(jax.random.fold_in(stream_key, 1), shape, 0, int(table[amount - 1]))
    grade = jnp.searchsorted(jnp.asarray(table, jnp.int32), lot, side="right")
    return jax.random.permutation(jax.random.fold_in(stream_key, 2), amount)[grade].astype(jnp.int32)


def split_up(count, total, reach, slope):
    weights = [(1 << 20) // math.isqrt(rank ** slope) + 1 for rank in range(2, count + 1)]
    spare, counts = total - reach - (count - 1), [1] * (count - 1)
    while spare > 0:
        candidates = [i for i in range(count - 1) if counts[i] < reach]
        pool, budget = sum([weights[i] for i in candidates]), spare
        for i in candidates:
            more = min(reach - counts[i], max(1, budget * weights[i] // pool), spare)
            counts[i] = counts[i] + more
            spare = spare - more
    return np.array([reach] + counts)


def ragged(stream_key, number_of, total, reach, lean):
    if number_of == 2:
        one = jax.random.randint(stream_key, (), max(1, total - reach), min(reach, total - 1) + 1)
        return jnp.stack([one, total - one])
    sizes = jnp.asarray(split_up(number_of, total, reach, lean), jnp.int32)
    twos = (number_of - 1) // 2
    source_of, sink = sizes[1:1 + 2 * twos:2], sizes[2:2 + 2 * twos:2]
    margin = jnp.minimum(source_of - 1, reach - sink)
    passed = jax.random.randint(jax.random.fold_in(stream_key, 1), (twos,), 0, 1 << 20) % (margin + 1)
    sizes = sizes.at[1:1 + 2 * twos:2].set(source_of - passed).at[2:2 + 2 * twos:2].set(sink + passed)
    return sizes[jax.random.permutation(jax.random.fold_in(stream_key, 2), number_of)]


def bell_draw(key, shape, deviation, limit, shards=(), kind=jnp.bfloat16):
    loudness = steps_of(key, shape, shards, -0.22, 0.18) if shards else 1.0
    array = jax.random.normal(key, shape, jnp.float32) * deviation * loudness
    return jnp.minimum(jnp.maximum(array, -limit), limit).astype(kind)


def setup_inputs(seed: int = 0) -> dict:
    key_of = jax.random.split(jax.random.key(seed), 8)
    return {
        "tokens": bell_draw(key_of[0], (TOKEN_COUNT, MODEL_WIDTH), 1.0, 6.0, ((0, 1024),)),
        "base_weight": bell_draw(key_of[1], (MODEL_WIDTH, VALUE_FEATURES), MODEL_WIDTH ** -0.5, 0.0625, ((0, 8),)),
        "adapter_down": bell_draw(key_of[2], (TENANTS, MODEL_WIDTH, R), MODEL_WIDTH ** -0.5, 0.0625, ((0, 128), (1, 8))),
        "adapter_up": bell_draw(key_of[3], (TENANTS, R, VALUE_FEATURES), R ** -0.5, 1.5, ((0, 128), (2, 8))),
        "upstream": bell_draw(key_of[4], (TOKEN_COUNT, VALUE_FEATURES), 0.5, 3.0, ((0, 128), (1, 8))),
        "block_tenant_index": place_ends(ranked_ids(key_of[5], (NBLOCKS,), TENANTS, 2), jax.random.fold_in(key_of[5], 3), 0, TENANTS - 1).astype(jnp.int32),
        "valid_lengths": ragged(key_of[6], NBLOCKS, NBLOCKS * BLOCK * 3 // 4, BLOCK, 0).astype(jnp.int32),
    }


adapter_scale = 2.0


def reference(tokens, base_weight, adapter_down, adapter_up, upstream, block_tenant_index, valid_lengths):
    width = MODEL_WIDTH // N_TP
    base_output = jnp.zeros((TOKEN_COUNT, VALUE_FEATURES), jnp.float32)
    for shard_index in range(N_TP):
        partial_value = jnp.dot(tokens[:, shard_index * width:(shard_index + 1) * width], base_weight[shard_index * width:(shard_index + 1) * width, :], preferred_element_type=jnp.float32)
        base_output = base_output + lax.optimization_barrier(partial_value.astype(jnp.bfloat16)).astype(jnp.float32)
    base_gradient = jnp.dot(upstream, base_weight.T, preferred_element_type=jnp.float32)
    blocked_tokens = tokens.reshape(NBLOCKS, BLOCK, MODEL_WIDTH)
    blocked_upstream_gradient = upstream.reshape(NBLOCKS, BLOCK, VALUE_FEATURES)

    def block_results(inputs):
        block_tokens, block_upstream_gradient, tenant, length = inputs
        down_factor = lax.dynamic_index_in_dim(adapter_down, tenant, 0, keepdims=False)
        up_weight_factor = lax.dynamic_index_in_dim(adapter_up, tenant, 0, keepdims=False)
        valid_tokens = (jnp.arange(BLOCK, dtype=jnp.int32) < length).astype(jnp.float32)[:, None]
        low_rank_state = jnp.dot(block_tokens, down_factor, preferred_element_type=jnp.float32).astype(jnp.bfloat16)
        backward_term = jnp.dot(block_upstream_gradient, up_weight_factor.T, preferred_element_type=jnp.float32).astype(jnp.bfloat16)
        adapter_output = adapter_scale * valid_tokens * jnp.dot(low_rank_state, up_weight_factor, preferred_element_type=jnp.float32)
        adapter_gradient = adapter_scale * valid_tokens * jnp.dot(backward_term, down_factor.T, preferred_element_type=jnp.float32)
        masked_tokens = jnp.where(valid_tokens > 0.0, low_rank_state, jnp.zeros_like(low_rank_state))
        adapter_contribution = adapter_scale * jnp.dot(masked_tokens.T, block_upstream_gradient, preferred_element_type=jnp.float32)
        return adapter_output, adapter_gradient, adapter_contribution

    adapter_output, adapter_gradient, adapter_contribution = lax.map(block_results, (blocked_tokens, blocked_upstream_gradient, block_tenant_index.astype(jnp.int32), valid_lengths.astype(jnp.int32)))
    projected = (base_output + adapter_output.reshape(TOKEN_COUNT, VALUE_FEATURES)).astype(jnp.bfloat16)
    activation_gradient = (base_gradient + adapter_gradient.reshape(TOKEN_COUNT, MODEL_WIDTH)).astype(jnp.bfloat16)
    up_grad = jax.ops.segment_sum(adapter_contribution, block_tenant_index.astype(jnp.int32), num_segments=TENANTS)
    return projected, activation_gradient, up_grad
```

```python
import functools

import jax
import jax.numpy as jnp
from jax import lax
from jax.experimental import pallas as pl
from jax.experimental.pallas import tpu as pltpu
from jax.sharding import Mesh
from jax.sharding import PartitionSpec as P

adapter_scale = 2.0
VMEM = pl.BlockSpec(memory_space=pltpu.VMEM)
SMEM = pl.BlockSpec(memory_space=pltpu.SMEM)
ANY = pl.BlockSpec(memory_space=pl.ANY)
REP = ("xlo", "far", "near", "core")


def params(mib=24):
    return pltpu.CompilerParams(vmem_limit_bytes=mib * 1024 * 1024)


def cost(flops, moved):
    return pl.CostEstimate(flops=flops, bytes_accessed=moved, transcendentals=0)


def struct(shape, dtype):
    return jax.ShapeDtypeStruct(shape, dtype)


def whole(shape):
    return pl.BlockSpec(shape, lambda i: (0,) * len(shape))


def dot(a, b, ca, cb):
    return lax.dot_general(
        a, b, (((ca,), (cb,)), ((), ())), preferred_element_type=jnp.float32
    )


def split_place(index, sizes):
    xlo_n, far_n, near_n, core_n = sizes
    core = lax.rem(index, core_n)
    index = lax.div(index, core_n)
    near = lax.rem(index, near_n)
    index = lax.div(index, near_n)
    return lax.div(index, far_n), lax.rem(index, far_n), near, core


def slab_kernel(parts, tokens_ref, upstream_ref, out_ref, held_ref, sems):
    rows, features = tokens_ref.shape[0], upstream_ref.shape[1]
    width = tokens_ref.shape[1] // parts
    slices = [
        pltpu.make_async_copy(
            tokens_ref.at[:, pl.ds(s * width, width)],
            out_ref.at[s, pl.ds(0, rows), :],
            sems.at[0, s],
        )
        for s in range(parts)
    ]
    folds = [
        pltpu.make_async_copy(
            upstream_ref.at[pl.ds(g * rows, rows), :],
            held_ref.at[:, pl.ds(g * features, features)],
            sems.at[1, g],
        )
        for g in range(parts)
    ]
    for copy in folds + slices:
        copy.start()
    for copy in folds:
        copy.wait()
    sends = [
        pltpu.make_async_copy(held_ref, out_ref.at[s, pl.ds(rows, rows), :], sems.at[2, s])
        for s in range(parts)
    ]
    for copy in sends:
        copy.start()
    for copy in slices + sends:
        copy.wait()


def table_kernel(sizes, place_ref, tenants_ref, held_ref, other_ref, out_ref, sems):
    xlo_n, far_n, near_n, core_n = sizes
    _, far, _, core = split_place(place_ref[0], sizes)
    for xlo in range(xlo_n):
        for near in range(near_n):
            block = ((xlo * far_n + far) * near_n + near) * core_n + core
            _, source_far, _, source_core = split_place(tenants_ref[block], sizes)
            slot = xlo * near_n + near

            @pl.when(source_core == core)
            def _():
                pltpu.make_async_copy(
                    held_ref.at[source_far], out_ref.at[slot], sems.at[slot]
                ).start()

            @pl.when(source_core != core)
            def _():
                pltpu.make_async_copy(
                    other_ref.at[source_far], out_ref.at[slot], sems.at[slot]
                ).start()

    for slot in range(xlo_n * near_n):
        pltpu.make_async_copy(held_ref.at[0], out_ref.at[slot], sems.at[slot]).wait()


def value_kernel(columns_ref, weight_ref, out_ref):
    sources, rows, width = columns_ref.shape
    columns = columns_ref[...].reshape(sources * rows, width)
    part = dot(columns, weight_ref[...], 1, 0).astype(jnp.bfloat16)
    parts, _, features = out_ref.shape
    for s in range(parts):
        out_ref[s] = part[:, s * features : (s + 1) * features]


def low_kernel(
    sizes,
    place_ref,
    tenants_ref,
    offered_ref,
    arrived_ref,
    upstream_ref,
    _,
    out_ref,
    item_ref,
    sem,
):
    xlo, _, near, _ = split_place(tenants_ref[place_ref[0]], sizes)
    copy = pltpu.make_async_copy(offered_ref.at[xlo * sizes[2] + near], item_ref, sem)
    copy.start()
    copy.wait()
    sources, rows, width = arrived_ref.shape[0], arrived_ref.shape[1] // 2, arrived_ref.shape[2]
    columns = arrived_ref[:, :rows, :].reshape(sources * rows, width)
    low = dot(item_ref[:, :width], columns, 1, 1)
    back = dot(item_ref[:, width:], upstream_ref[...], 1, 1)
    both = jnp.concatenate([low, back], axis=0).astype(jnp.bfloat16)
    ranks, lanes = both.shape[0], out_ref.shape[2]
    for s in range(out_ref.shape[0]):
        for g in range(both.shape[1] // lanes):
            out_ref[s, g * ranks : (g + 1) * ranks, :] = both[:, g * lanes : (g + 1) * lanes]


def rank_kernel(place_ref, lengths_ref, parts_ref, upstream_ref, both_ref, out_ref):
    length = lengths_ref[place_ref[0]]
    total = parts_ref[0].astype(jnp.float32)
    for s in range(1, parts_ref.shape[0]):
        total = total + parts_ref[s].astype(jnp.float32)
    ranks = both_ref.shape[0]
    total = jnp.concatenate(
        [total[g * ranks : (g + 1) * ranks] for g in range(total.shape[0] // ranks)], axis=1
    )
    total = total.astype(jnp.bfloat16).astype(jnp.float32)
    live = lax.broadcasted_iota(jnp.int32, total.shape, 1) < length
    both = jnp.where(live, adapter_scale * total, 0.0).astype(jnp.bfloat16)
    both_ref[...] = both
    mine = dot(both[: ranks // 2], upstream_ref[...], 1, 0)
    for member in range(out_ref.shape[0]):
        out_ref[member] = mine


def route_kernel(sizes, place_ref, tenants_ref, parts_ref, out_ref, total_ref):
    xlo_n, far_n, near_n, core_n = sizes
    my_xlo, far, near, my_core = split_place(place_ref[0], sizes)
    total_ref[...] = jnp.zeros_like(total_ref)
    for xlo in range(xlo_n):
        for core in range(core_n):
            block = ((xlo * far_n + far) * near_n + near) * core_n + core
            to_xlo, to_far, to_near, to_core = split_place(tenants_ref[block], sizes)

            @pl.when((to_xlo == my_xlo) & (to_core == my_core))
            def _():
                total_ref[to_far * near_n + to_near] += parts_ref[xlo * core_n + core]

    out_ref[...] = total_ref[...].astype(out_ref.dtype)


def sum_kernel(parts_ref, out_ref):
    total = parts_ref[0].astype(jnp.float32)
    for s in range(1, parts_ref.shape[0]):
        total = total + parts_ref[s].astype(jnp.float32)
    out_ref[0] = total


def projected_kernel(width, parts_ref, both_ref, item_ref, out_ref):
    rank = item_ref.shape[0]
    total = parts_ref[0].astype(jnp.float32)
    for s in range(1, parts_ref.shape[0]):
        total = total + parts_ref[s].astype(jnp.float32)
    term = dot(both_ref[:rank], item_ref[:, width:], 0, 0)
    out_ref[...] = (total + term).astype(jnp.bfloat16)


def gradient_kernel(upstream_ref, weight_ref, both_ref, item_ref, out_ref):
    rank, width = item_ref.shape[0], weight_ref.shape[0]
    sources, _, lanes = upstream_ref.shape
    features = weight_ref.shape[1] // sources
    rows = jnp.concatenate(
        [
            jnp.concatenate(
                [upstream_ref[s, :, at : at + features] for s in range(sources)], axis=1
            )
            for at in range(0, lanes, features)
        ],
        axis=0,
    )
    total = dot(rows, weight_ref[...], 1, 1)
    total = total + dot(both_ref[rank:], item_ref[:, :width], 0, 0)
    out_ref[...] = total.astype(jnp.bfloat16)


def on_device(
    sizes, parts, tokens, base_weight, adapter_down, adapter_up, upstream, tenants, lengths
):
    bf16, f32 = jnp.bfloat16, jnp.float32
    xlo_n, far_n, near_n, core_n = sizes
    place = lax.axis_index(REP).astype(jnp.int32).reshape(1)
    rows, full_width = tokens.shape
    width = full_width // parts
    block, features = upstream.shape
    rank = adapter_up.shape[1]
    values = base_weight.shape[1]
    row_step = 128
    rank_rows = 2 * rank * block // features
    sent_rows = block + rank_rows

    slabs = pl.pallas_call(
        functools.partial(slab_kernel, parts),
        out_shape=struct((parts, 2 * rows, width), bf16),
        in_specs=[ANY, ANY],
        out_specs=ANY,
        scratch_shapes=[
            pltpu.VMEM((rows, width), bf16),
            pltpu.SemaphoreType.DMA((3, parts)),
        ],
        compiler_params=params(),
        name="slab",
    )(tokens, upstream)
    arrived = lax.all_to_all(slabs, "tp", 0, 0, tiled=True)

    own = jnp.concatenate([adapter_down[0].T, adapter_up[0]], axis=1)
    held = lax.all_gather(own, "far", axis=0, tiled=False)
    other = lax.ppermute(held, "core", [(c, (c + 1) % core_n) for c in range(core_n)])

    value_parts = pl.pallas_call(
        value_kernel,
        grid=(block // row_step,),
        out_shape=struct((parts, sent_rows, features), bf16),
        in_specs=[
            pl.BlockSpec((row_step // rows, rows, width), lambda i: (i, 0, 0)),
            pl.BlockSpec((width, values), lambda i: (0, 0)),
        ],
        out_specs=pl.BlockSpec((parts, row_step, features), lambda i: (0, i, 0)),
        compiler_params=params(),
        cost_estimate=cost(2 * block * width * values, 4 << 20),
        name="value",
    )(arrived, base_weight)

    table = pl.pallas_call(
        functools.partial(table_kernel, sizes),
        out_shape=struct((xlo_n * near_n,) + own.shape, bf16),
        in_specs=[SMEM, SMEM, ANY, ANY],
        out_specs=ANY,
        scratch_shapes=[pltpu.SemaphoreType.DMA((xlo_n * near_n,))],
        compiler_params=params(),
        name="table",
    )(place, tenants, held, other)
    offered = lax.all_to_all(table, ("xlo", "near"), 0, 0, tiled=True)

    sent, item = pl.pallas_call(
        functools.partial(low_kernel, sizes),
        grid=(1,),
        out_shape=(struct((parts, sent_rows, features), bf16), struct(own.shape, bf16)),
        in_specs=[SMEM, SMEM, ANY, VMEM, VMEM, ANY],
        out_specs=(
            pl.BlockSpec((parts, rank_rows, features), lambda i: (0, block // rank_rows, 0)),
            whole(own.shape),
        ),
        scratch_shapes=[pltpu.SemaphoreType.DMA],
        input_output_aliases={5: 0},
        compiler_params=params(),
        name="low",
    )(place, tenants, offered, arrived, upstream, value_parts)
    back = lax.all_to_all(sent, "tp", 0, 0, tiled=True)

    rank_spec = pl.BlockSpec(
        (parts, rank_rows, features), lambda i: (0, block // rank_rows, 0)
    )
    both, mine = pl.pallas_call(
        rank_kernel,
        grid=(1,),
        out_shape=(
            struct((2 * rank, block), bf16),
            struct((xlo_n * core_n, rank, features), f32),
        ),
        in_specs=[SMEM, SMEM, rank_spec, VMEM],
        out_specs=(
            whole((2 * rank, block)),
            whole((xlo_n * core_n, rank, features)),
        ),
        compiler_params=params(),
        name="rank",
    )(place, lengths, back, upstream)
    near_parts = lax.all_to_all(mine, ("xlo", "core"), 0, 0, tiled=True)
    routed = pl.pallas_call(
        functools.partial(route_kernel, sizes),
        grid=(1,),
        out_shape=struct((far_n * near_n, rank, features), bf16),
        in_specs=[SMEM, SMEM, whole((xlo_n * core_n, rank, features))],
        out_specs=whole((far_n * near_n, rank, features)),
        scratch_shapes=[pltpu.VMEM((far_n * near_n, rank, features), f32)],
        compiler_params=params(),
        name="route",
    )(place, tenants, near_parts)
    far_parts = lax.all_to_all(routed, ("far", "near"), 0, 0, tiled=True)
    up_grad = pl.pallas_call(
        sum_kernel,
        grid=(1,),
        out_shape=struct((1, rank, features), f32),
        in_specs=[whole((far_n * near_n, rank, features))],
        out_specs=whole((1, rank, features)),
        compiler_params=params(),
        name="total",
    )(far_parts)

    gradient = pl.pallas_call(
        gradient_kernel,
        grid=(block // row_step,),
        out_shape=struct((block, width), bf16),
        in_specs=[
            pl.BlockSpec(
                (parts, rows, row_step // rows * features), lambda i: (0, 1, i)
            ),
            pl.BlockSpec((width, values), lambda i: (0, 0)),
            pl.BlockSpec((2 * rank, row_step), lambda i: (0, i)),
            pl.BlockSpec(own.shape, lambda i: (0, 0)),
        ],
        out_specs=pl.BlockSpec((row_step, width), lambda i: (i, 0)),
        compiler_params=params(),
        cost_estimate=cost(2 * block * width * values, 4 << 20),
        name="gradient",
    )(arrived, base_weight, both, item)
    projected = pl.pallas_call(
        functools.partial(projected_kernel, width),
        grid=(1,),
        out_shape=struct((block, features), bf16),
        in_specs=[
            pl.BlockSpec((parts, block, features), lambda i: (0, 0, 0)),
            whole((2 * rank, block)),
            whole(own.shape),
        ],
        out_specs=whole((block, features)),
        compiler_params=params(),
        name="projected",
    )(back, both, item)
    return projected, gradient, up_grad


def solution(mesh):
    replicas, parts = mesh.devices.shape
    cores, xlo, near = 2, 2, 4
    sizes = (xlo, replicas // (xlo * near * cores), near, cores)
    fine = Mesh(mesh.devices.reshape(sizes + (parts,)), REP + ("tp",))
    return jax.shard_map(
        functools.partial(on_device, sizes, parts),
        mesh=fine,
        in_specs=(
            P(REP + ("tp",), None),
            P("tp", None),
            P(REP, "tp", None),
            P(REP, None, "tp"),
            P(REP, "tp"),
            P(),
            P(),
        ),
        out_specs=(P(REP, "tp"), P(REP, "tp"), P(REP, None, "tp")),
        check_vma=False,
    )
```

```python
import functools

import jax
import jax.numpy as jnp
from jax import lax
from jax.experimental import pallas as pl
from jax.experimental.pallas import tpu as pltpu
from jax.sharding import Mesh
from jax.sharding import PartitionSpec as P

adapter_scale = 2.0
VMEM = pl.BlockSpec(memory_space=pltpu.VMEM)
SMEM = pl.BlockSpec(memory_space=pltpu.SMEM)
ANY = pl.BlockSpec(memory_space=pl.ANY)
HBM = pl.BlockSpec(memory_space=pltpu.HBM)
REP = ("xlo", "far", "near", "core")


def params(mib=8):
    return pltpu.CompilerParams(vmem_limit_bytes=mib * 1024 * 1024)


def cost(flops, moved):
    return pl.CostEstimate(flops=flops, bytes_accessed=moved, transcendentals=0)


def struct(shape, dtype):
    return jax.ShapeDtypeStruct(shape, dtype)


def whole(shape):
    return pl.BlockSpec(shape, lambda i: (0,) * len(shape))


def dot(a, b, ca, cb):
    return lax.dot_general(
        a, b, (((ca,), (cb,)), ((), ())), preferred_element_type=jnp.float32
    )


def split_place(index, sizes):
    xlo_n, far_n, near_n, core_n = sizes
    core = lax.rem(index, core_n)
    index = lax.div(index, core_n)
    near = lax.rem(index, near_n)
    index = lax.div(index, near_n)
    return lax.div(index, far_n), lax.rem(index, far_n), near, core


def slab_kernel(parts, tokens_ref, upstream_ref, out_ref, held_ref, sems):
    rows, features = tokens_ref.shape[0], upstream_ref.shape[1]
    width = tokens_ref.shape[1] // parts
    slices = [
        pltpu.make_async_copy(
            tokens_ref.at[:, pl.ds(s * width, width)],
            out_ref.at[s, pl.ds(0, rows), :],
            sems.at[0, s],
        )
        for s in range(parts)
    ]
    folds = [
        pltpu.make_async_copy(
            upstream_ref.at[pl.ds(g * rows, rows), :],
            held_ref.at[:, pl.ds(g * features, features)],
            sems.at[1, g],
        )
        for g in range(parts)
    ]
    for copy in folds + slices:
        copy.start()
    for copy in folds:
        copy.wait()
    sends = [
        pltpu.make_async_copy(held_ref, out_ref.at[s, pl.ds(rows, rows), :], sems.at[2, s])
        for s in range(parts)
    ]
    for copy in sends:
        copy.start()
    for copy in slices + sends:
        copy.wait()


def table_kernel(sizes, place_ref, tenants_ref, held_ref, other_ref, out_ref, sems):
    xlo_n, far_n, near_n, core_n = sizes
    _, far, _, core = split_place(place_ref[0], sizes)
    for xlo in range(xlo_n):
        for near in range(near_n):
            block = ((xlo * far_n + far) * near_n + near) * core_n + core
            _, source_far, _, source_core = split_place(tenants_ref[block], sizes)
            slot = xlo * near_n + near

            @pl.when(source_core == core)
            def _():
                pltpu.make_async_copy(
                    held_ref.at[source_far], out_ref.at[slot], sems.at[slot]
                ).start()

            @pl.when(source_core != core)
            def _():
                pltpu.make_async_copy(
                    other_ref.at[source_far], out_ref.at[slot], sems.at[slot]
                ).start()

    for slot in range(xlo_n * near_n):
        pltpu.make_async_copy(held_ref.at[0], out_ref.at[slot], sems.at[slot]).wait()


def value_kernel(columns_ref, weight_ref, *refs):
    outs, held_ref = refs[:-1], refs[-1]
    sources, rows, width = columns_ref.shape
    columns = columns_ref[...].reshape(sources * rows, width)
    held_ref[...] = dot(columns, weight_ref[...], 1, 0).astype(jnp.bfloat16)
    me, parts, features = lax.axis_index("tp"), len(outs), outs[0].shape[1]
    for k, out_ref in enumerate(outs):
        at = pl.multiple_of(lax.rem(me + k, parts) * features, features)
        out_ref[...] = held_ref[:, pl.ds(at, features)]


def low_kernel(
    sizes,
    place_ref,
    tenants_ref,
    offered_ref,
    arrived_ref,
    upstream_ref,
    out_ref,
    item_ref,
    sem,
):
    xlo, _, near, _ = split_place(tenants_ref[place_ref[0]], sizes)
    copy = pltpu.make_async_copy(offered_ref.at[xlo * sizes[2] + near], item_ref, sem)
    copy.start()
    copy.wait()
    sources, rows, width = arrived_ref.shape[0], arrived_ref.shape[1] // 2, arrived_ref.shape[2]
    columns = arrived_ref[:, :rows, :].reshape(sources * rows, width)
    low = dot(item_ref[:, :width], columns, 1, 1)
    back = dot(item_ref[:, width:], upstream_ref[...], 1, 1)
    both = jnp.concatenate([low, back], axis=0).astype(jnp.bfloat16)
    for s in range(out_ref.shape[0]):
        out_ref[s] = both


def rank_kernel(place_ref, lengths_ref, parts_ref, upstream_ref, both_ref, out_ref):
    length = lengths_ref[place_ref[0]]
    total = parts_ref[0].astype(jnp.float32)
    for s in range(1, parts_ref.shape[0]):
        total = total + parts_ref[s].astype(jnp.float32)
    ranks = both_ref.shape[0]
    total = total.astype(jnp.bfloat16).astype(jnp.float32)
    live = lax.broadcasted_iota(jnp.int32, total.shape, 1) < length
    both = jnp.where(live, adapter_scale * total, 0.0).astype(jnp.bfloat16)
    both_ref[...] = both
    mine = dot(both[: ranks // 2], upstream_ref[...], 1, 0)
    for member in range(out_ref.shape[0]):
        out_ref[member] = mine


def route_kernel(sizes, place_ref, tenants_ref, parts_ref, *refs):
    out_ref, total_ref = refs[-2:]
    xlo_n, far_n, near_n, core_n = sizes
    my_xlo, far, near, my_core = split_place(place_ref[0], sizes)
    total_ref[...] = jnp.zeros_like(total_ref)
    for xlo in range(xlo_n):
        for core in range(core_n):
            block = ((xlo * far_n + far) * near_n + near) * core_n + core
            to_xlo, to_far, to_near, to_core = split_place(tenants_ref[block], sizes)

            @pl.when((to_xlo == my_xlo) & (to_core == my_core))
            def _():
                total_ref[to_far * near_n + to_near] += parts_ref[xlo * core_n + core]

    out_ref[...] = total_ref[...].astype(out_ref.dtype)


def sum_kernel(parts_ref, out_ref):
    total = parts_ref[0].astype(jnp.float32)
    for s in range(1, parts_ref.shape[0]):
        total = total + parts_ref[s].astype(jnp.float32)
    out_ref[0] = total


def projected_kernel(width, both_ref, item_ref, *refs):
    rank, out_ref = item_ref.shape[0], refs[-1]
    total = refs[0][...].astype(jnp.float32)
    for part_ref in refs[1:-1]:
        total = total + part_ref[...].astype(jnp.float32)
    term = dot(both_ref[:rank], item_ref[:, width:], 0, 0)
    out_ref[...] = (total + term).astype(jnp.bfloat16)


def gradient_kernel(upstream_ref, weight_ref, both_ref, item_ref, out_ref):
    rank, width = item_ref.shape[0], weight_ref.shape[0]
    sources, _, lanes = upstream_ref.shape
    features = weight_ref.shape[1] // sources
    rows = jnp.concatenate(
        [
            jnp.concatenate(
                [upstream_ref[s, :, at : at + features] for s in range(sources)], axis=1
            )
            for at in range(0, lanes, features)
        ],
        axis=0,
    )
    total = dot(rows, weight_ref[...], 1, 1)
    total = total + dot(both_ref[rank:], item_ref[:, :width], 0, 0)
    out_ref[...] = total.astype(jnp.bfloat16)


def on_device(
    sizes, parts, tokens, base_weight, adapter_down, adapter_up, upstream, tenants, lengths
):
    bf16, f32 = jnp.bfloat16, jnp.float32
    xlo_n, far_n, near_n, core_n = sizes
    place = lax.axis_index(REP).astype(jnp.int32).reshape(1)
    rows, full_width = tokens.shape
    width = full_width // parts
    block, features = upstream.shape
    rank = adapter_up.shape[1]
    values = base_weight.shape[1]
    row_step = 128
    slabs = pl.pallas_call(
        functools.partial(slab_kernel, parts),
        out_shape=struct((parts, 2 * rows, width), bf16),
        in_specs=[HBM, HBM],
        out_specs=HBM,
        scratch_shapes=[
            pltpu.VMEM((rows, width), bf16),
            pltpu.SemaphoreType.DMA((3, parts)),
        ],
        compiler_params=params(60),
        name="slab",
    )(tokens, upstream)
    arrived = lax.all_to_all(slabs, "tp", 0, 0, tiled=True)

    own = jnp.concatenate([adapter_down[0].T, adapter_up[0]], axis=1)
    held = lax.all_gather(own, "far", axis=0, tiled=False)
    other = lax.ppermute(held, "core", [(c, (c + 1) % core_n) for c in range(core_n)])

    value_parts = pl.pallas_call(
        value_kernel,
        grid=(block // row_step,),
        out_shape=[struct((block, features), bf16)] * parts,
        in_specs=[
            pl.BlockSpec((row_step // rows, rows, width), lambda i: (i, 0, 0)),
            pl.BlockSpec((width, values), lambda i: (0, 0)),
        ],
        out_specs=[pl.BlockSpec((row_step, features), lambda i: (i, 0))] * parts,
        scratch_shapes=[pltpu.VMEM((row_step, values), bf16)],
        compiler_params=params(12),
        cost_estimate=cost(2 * block * width * values, 4 << 20),
        name="value",
    )(arrived, base_weight)

    table = pl.pallas_call(
        functools.partial(table_kernel, sizes),
        out_shape=struct((xlo_n * near_n,) + own.shape, bf16),
        in_specs=[SMEM, SMEM, ANY, ANY],
        out_specs=ANY,
        scratch_shapes=[pltpu.SemaphoreType.DMA((xlo_n * near_n,))],
        compiler_params=params(),
        name="table",
    )(place, tenants, held, other)
    offered = lax.all_to_all(table, ("xlo", "near"), 0, 0, tiled=True)

    sent, item = pl.pallas_call(
        functools.partial(low_kernel, sizes),
        grid=(1,),
        out_shape=(struct((parts, 2 * rank, block), bf16), struct(own.shape, bf16)),
        in_specs=[SMEM, SMEM, ANY, VMEM, VMEM],
        out_specs=(whole((parts, 2 * rank, block)), whole(own.shape)),
        scratch_shapes=[pltpu.SemaphoreType.DMA],
        compiler_params=params(),
        name="low",
    )(place, tenants, offered, arrived, upstream)
    back = lax.all_to_all(sent, "tp", 0, 0, tiled=True)

    both, mine = pl.pallas_call(
        rank_kernel,
        grid=(1,),
        out_shape=(
            struct((2 * rank, block), bf16),
            struct((xlo_n * core_n, rank, features), f32),
        ),
        in_specs=[SMEM, SMEM, whole((parts, 2 * rank, block)), VMEM],
        out_specs=(
            whole((2 * rank, block)),
            whole((xlo_n * core_n, rank, features)),
        ),
        compiler_params=params(),
        name="rank",
    )(place, lengths, back, upstream)
    near_parts = lax.all_to_all(mine, ("xlo", "core"), 0, 0, tiled=True)
    *value_parts, routed = pl.pallas_call(
        functools.partial(route_kernel, sizes),
        grid=(1,),
        out_shape=[struct((block, features), bf16)] * parts
        + [struct((far_n * near_n, rank, features), bf16)],
        in_specs=[SMEM, SMEM, whole((xlo_n * core_n, rank, features))] + [ANY] * parts,
        out_specs=[ANY] * parts + [whole((far_n * near_n, rank, features))],
        scratch_shapes=[pltpu.VMEM((far_n * near_n, rank, features), f32)],
        input_output_aliases={3 + k: k for k in range(parts)},
        compiler_params=params(),
        name="route",
    )(place, tenants, near_parts, *value_parts)
    far_parts = lax.all_to_all(routed, ("far", "near"), 0, 0, tiled=True)
    value_sums = [value_parts[0]] + [
        lax.ppermute(value_parts[k], "tp", [(d, (d + k) % parts) for d in range(parts)])
        for k in range(1, parts)
    ]
    up_grad = pl.pallas_call(
        sum_kernel,
        grid=(1,),
        out_shape=struct((1, rank, features), f32),
        in_specs=[whole((far_n * near_n, rank, features))],
        out_specs=whole((1, rank, features)),
        compiler_params=params(),
        name="total",
    )(far_parts)

    gradient = pl.pallas_call(
        gradient_kernel,
        grid=(block // row_step,),
        out_shape=struct((block, width), bf16),
        in_specs=[
            pl.BlockSpec(
                (parts, rows, row_step // rows * features), lambda i: (0, 1, i)
            ),
            pl.BlockSpec((width, values), lambda i: (0, 0)),
            pl.BlockSpec((2 * rank, row_step), lambda i: (0, i)),
            pl.BlockSpec(own.shape, lambda i: (0, 0)),
        ],
        out_specs=pl.BlockSpec((row_step, width), lambda i: (i, 0)),
        compiler_params=params(12),
        cost_estimate=cost(2 * block * width * values, 4 << 20),
        name="gradient",
    )(arrived, base_weight, both, item)
    projected = pl.pallas_call(
        functools.partial(projected_kernel, width),
        grid=(1,),
        out_shape=struct((block, features), bf16),
        in_specs=[whole((2 * rank, block)), whole(own.shape)]
        + [whole((block, features))] * parts,
        out_specs=whole((block, features)),
        compiler_params=params(),
        name="projected",
    )(both, item, *value_sums)
    return projected, gradient, up_grad


def solution(mesh):
    replicas, parts = mesh.devices.shape
    cores, xlo, near = 2, 2, 4
    sizes = (xlo, replicas // (xlo * near * cores), near, cores)
    fine = Mesh(mesh.devices.reshape(sizes + (parts,)), REP + ("tp",))
    return jax.shard_map(
        functools.partial(on_device, sizes, parts),
        mesh=fine,
        in_specs=(
            P(REP + ("tp",), None),
            P("tp", None),
            P(REP, "tp", None),
            P(REP, None, "tp"),
            P(REP, "tp"),
            P(),
            P(),
        ),
        out_specs=(P(REP, "tp"), P(REP, "tp"), P(REP, None, "tp")),
        check_vma=False,
    )
```

```python
import functools

import jax
import jax.numpy as jnp
from jax import lax
from jax.experimental import pallas as pl
from jax.experimental.pallas import tpu as pltpu
from jax.sharding import Mesh
from jax.sharding import PartitionSpec as P

adapter_scale = 2.0
VMEM = pl.BlockSpec(memory_space=pltpu.VMEM)
SMEM = pl.BlockSpec(memory_space=pltpu.SMEM)
ANY = pl.BlockSpec(memory_space=pl.ANY)
HBM = pl.BlockSpec(memory_space=pltpu.HBM)
REP = ("xlo", "far", "near", "core")


def params(mib=8):
    return pltpu.CompilerParams(vmem_limit_bytes=mib * 1024 * 1024)


def cost(flops, moved):
    return pl.CostEstimate(flops=flops, bytes_accessed=moved, transcendentals=0)


def struct(shape, dtype):
    return jax.ShapeDtypeStruct(shape, dtype)


def whole(shape):
    return pl.BlockSpec(shape, lambda i: (0,) * len(shape))


def dot(a, b, ca, cb):
    return lax.dot_general(
        a, b, (((ca,), (cb,)), ((), ())), preferred_element_type=jnp.float32
    )


def split_place(index, sizes):
    xlo_n, far_n, near_n, core_n = sizes
    core = lax.rem(index, core_n)
    index = lax.div(index, core_n)
    near = lax.rem(index, near_n)
    index = lax.div(index, near_n)
    return lax.div(index, far_n), lax.rem(index, far_n), near, core


def slab_kernel(parts, tokens_ref, upstream_ref, out_ref, slices_ref, fold_ref, sems):
    rows, features = tokens_ref.shape[0], upstream_ref.shape[1]
    width = tokens_ref.shape[1] // parts
    folds = [
        pltpu.make_async_copy(
            upstream_ref.at[pl.ds(g * rows, rows), :],
            fold_ref.at[:, pl.ds(g * features, features)],
            sems.at[1, g],
        )
        for g in range(parts)
    ]
    slices = [
        pltpu.make_async_copy(
            tokens_ref.at[:, pl.ds(s * width, width)], slices_ref.at[s], sems.at[0, s]
        )
        for s in range(parts)
    ]
    for copy in folds + slices:
        copy.start()
    sends = []
    for copy in folds:
        copy.wait()
    for s in range(parts):
        sends.append(
            pltpu.make_async_copy(fold_ref, out_ref.at[s, pl.ds(rows, rows), :], sems.at[2, s])
        )
        sends[-1].start()
    for s in range(parts):
        slices[s].wait()
        sends.append(
            pltpu.make_async_copy(
                slices_ref.at[s], out_ref.at[s, pl.ds(0, rows), :], sems.at[3, s]
            )
        )
        sends[-1].start()
    for copy in sends:
        copy.wait()


def table_kernel(sizes, place_ref, tenants_ref, held_ref, other_ref, out_ref, sems):
    xlo_n, far_n, near_n, core_n = sizes
    _, far, _, core = split_place(place_ref[0], sizes)
    for xlo in range(xlo_n):
        for near in range(near_n):
            block = ((xlo * far_n + far) * near_n + near) * core_n + core
            _, source_far, _, source_core = split_place(tenants_ref[block], sizes)
            slot = xlo * near_n + near

            @pl.when(source_core == core)
            def _():
                pltpu.make_async_copy(
                    held_ref.at[source_far], out_ref.at[slot], sems.at[slot]
                ).start()

            @pl.when(source_core != core)
            def _():
                pltpu.make_async_copy(
                    other_ref.at[source_far], out_ref.at[slot], sems.at[slot]
                ).start()

    for slot in range(xlo_n * near_n):
        pltpu.make_async_copy(held_ref.at[0], out_ref.at[slot], sems.at[slot]).wait()


def value_kernel(columns_ref, weight_ref, *refs):
    outs, held_ref = refs[:-1], refs[-1]
    sources, rows, width = columns_ref.shape
    columns = columns_ref[...].reshape(sources * rows, width)
    held_ref[...] = dot(columns, weight_ref[...], 1, 0).astype(jnp.bfloat16)
    me, parts, features = lax.axis_index("tp"), len(outs), outs[0].shape[1]
    for k, out_ref in enumerate(outs):
        at = pl.multiple_of(lax.rem(me + k, parts) * features, features)
        out_ref[...] = held_ref[:, pl.ds(at, features)]


def low_kernel(
    sizes,
    place_ref,
    tenants_ref,
    offered_ref,
    arrived_ref,
    upstream_ref,
    *refs,
):
    out_ref, item_ref, sem = refs[-3:]
    xlo, _, near, _ = split_place(tenants_ref[place_ref[0]], sizes)
    copy = pltpu.make_async_copy(offered_ref.at[xlo * sizes[2] + near], item_ref, sem)
    copy.start()
    copy.wait()
    sources, rows, width = arrived_ref.shape[0], arrived_ref.shape[1] // 2, arrived_ref.shape[2]
    columns = arrived_ref[:, :rows, :].reshape(sources * rows, width)
    low = dot(item_ref[:, :width], columns, 1, 1)
    back = dot(item_ref[:, width:], upstream_ref[...], 1, 1)
    both = jnp.concatenate([low, back], axis=0).astype(jnp.bfloat16)
    for s in range(out_ref.shape[0]):
        out_ref[s] = both


def rank_kernel(place_ref, lengths_ref, parts_ref, upstream_ref, *refs):
    both_ref, out_ref = refs[-2:]
    length = lengths_ref[place_ref[0]]
    total = parts_ref[0].astype(jnp.float32)
    for s in range(1, parts_ref.shape[0]):
        total = total + parts_ref[s].astype(jnp.float32)
    ranks = both_ref.shape[0]
    total = total.astype(jnp.bfloat16).astype(jnp.float32)
    live = lax.broadcasted_iota(jnp.int32, total.shape, 1) < length
    both = jnp.where(live, adapter_scale * total, 0.0).astype(jnp.bfloat16)
    both_ref[...] = both
    mine = dot(both[: ranks // 2], upstream_ref[...], 1, 0)
    for member in range(out_ref.shape[0]):
        out_ref[member] = mine


def route_kernel(sizes, place_ref, tenants_ref, parts_ref, *refs):
    out_ref, total_ref = refs[-2:]
    xlo_n, far_n, near_n, core_n = sizes
    my_xlo, far, my_near, my_core = split_place(place_ref[0], sizes)
    total_ref[...] = jnp.zeros_like(total_ref)
    for xlo in range(xlo_n):
        for near in range(near_n):
            for core in range(core_n):
                block = ((xlo * far_n + far) * near_n + near) * core_n + core
                to_xlo, to_far, to_near, to_core = split_place(tenants_ref[block], sizes)
                member = (xlo * near_n + near) * core_n + core

                @pl.when((to_xlo == my_xlo) & (to_near == my_near) & (to_core == my_core))
                def _():
                    total_ref[to_far] += parts_ref[member]

    out_ref[...] = total_ref[...].astype(out_ref.dtype)


def sum_kernel(parts_ref, out_ref):
    total = parts_ref[0].astype(jnp.float32)
    for s in range(1, parts_ref.shape[0]):
        total = total + parts_ref[s].astype(jnp.float32)
    out_ref[0] = total


def projected_kernel(width, both_ref, item_ref, *refs):
    rank, out_ref = item_ref.shape[0], refs[-1]
    total = refs[0][...].astype(jnp.float32)
    for part_ref in refs[1:-1]:
        total = total + part_ref[...].astype(jnp.float32)
    term = dot(both_ref[:rank], item_ref[:, width:], 0, 0)
    out_ref[...] = (total + term).astype(jnp.bfloat16)


def gradient_kernel(upstream_ref, weight_ref, both_ref, item_ref, out_ref):
    rank, width = item_ref.shape[0], weight_ref.shape[0]
    sources, _, lanes = upstream_ref.shape
    features = weight_ref.shape[1] // sources
    rows = jnp.concatenate(
        [
            jnp.concatenate(
                [upstream_ref[s, :, at : at + features] for s in range(sources)], axis=1
            )
            for at in range(0, lanes, features)
        ],
        axis=0,
    )
    total = dot(rows, weight_ref[...], 1, 1)
    total = total + dot(both_ref[rank:], item_ref[:, :width], 0, 0)
    out_ref[...] = total.astype(jnp.bfloat16)


def on_device(
    sizes, parts, tokens, base_weight, adapter_down, adapter_up, upstream, tenants, lengths
):
    bf16, f32 = jnp.bfloat16, jnp.float32
    xlo_n, far_n, near_n, core_n = sizes
    place = lax.axis_index(REP).astype(jnp.int32).reshape(1)
    rows, full_width = tokens.shape
    width = full_width // parts
    block, features = upstream.shape
    rank = adapter_up.shape[1]
    values = base_weight.shape[1]
    row_step = 128
    slabs = pl.pallas_call(
        functools.partial(slab_kernel, parts),
        out_shape=struct((parts, 2 * rows, width), bf16),
        in_specs=[HBM, HBM],
        out_specs=HBM,
        scratch_shapes=[
            pltpu.VMEM((parts, rows, width), bf16),
            pltpu.VMEM((rows, width), bf16),
            pltpu.SemaphoreType.DMA((4, parts)),
        ],
        compiler_params=params(60),
        name="slab",
    )(tokens, upstream)
    arrived = lax.all_to_all(slabs, "tp", 0, 0, tiled=True)

    own = jnp.concatenate([adapter_down[0].T, adapter_up[0]], axis=1)
    held = lax.all_gather(own, "far", axis=0, tiled=False)
    other = lax.ppermute(held, "core", [(c, (c + 1) % core_n) for c in range(core_n)])

    value_parts = pl.pallas_call(
        value_kernel,
        grid=(block // row_step,),
        out_shape=[struct((block, features), bf16)] * parts,
        in_specs=[
            pl.BlockSpec((row_step // rows, rows, width), lambda i: (i, 0, 0)),
            pl.BlockSpec((width, values), lambda i: (0, 0)),
        ],
        out_specs=[pl.BlockSpec((row_step, features), lambda i: (i, 0))] * parts,
        scratch_shapes=[pltpu.VMEM((row_step, values), bf16)],
        compiler_params=params(12),
        cost_estimate=cost(2 * block * width * values, 4 << 20),
        name="value",
    )(arrived, base_weight)

    table = pl.pallas_call(
        functools.partial(table_kernel, sizes),
        out_shape=struct((xlo_n * near_n,) + own.shape, bf16),
        in_specs=[SMEM, SMEM, ANY, ANY],
        out_specs=ANY,
        scratch_shapes=[pltpu.SemaphoreType.DMA((xlo_n * near_n,))],
        compiler_params=params(),
        name="table",
    )(place, tenants, held, other)
    offered = lax.all_to_all(table, ("xlo", "near"), 0, 0, tiled=True)

    early, middle, late, last = (1, 2), (3, 4), (5,), (6, 7)
    parcels = [struct((block, features), bf16)]
    sums = [value_parts[0]]

    def leave(buffers, hops):
        return [
            lax.ppermute(buffer, "tp", [(d, (d + k) % parts) for d in range(parts)])
            for buffer, k in zip(buffers, hops)
        ]

    came = leave([value_parts[k] for k in early], early)
    ahead = came + [value_parts[k] for k in middle]
    *ahead, sent, item = pl.pallas_call(
        functools.partial(low_kernel, sizes),
        grid=(1,),
        out_shape=parcels * len(ahead)
        + [struct((parts, 2 * rank, block), bf16), struct(own.shape, bf16)],
        in_specs=[SMEM, SMEM, ANY, VMEM, VMEM] + [ANY] * len(ahead),
        out_specs=[ANY] * len(ahead) + [whole((parts, 2 * rank, block)), whole(own.shape)],
        scratch_shapes=[pltpu.SemaphoreType.DMA],
        input_output_aliases={5 + k: k for k in range(len(ahead))},
        compiler_params=params(),
        name="low",
    )(place, tenants, offered, arrived, upstream, *ahead)
    sums += ahead[: len(early)]
    back = lax.all_to_all(sent, "tp", 0, 0, tiled=True)

    came = leave(ahead[len(early) :], middle)
    ahead = came + [value_parts[k] for k in late]
    *ahead, both, mine = pl.pallas_call(
        rank_kernel,
        grid=(1,),
        out_shape=parcels * len(ahead)
        + [
            struct((2 * rank, block), bf16),
            struct((xlo_n * near_n * core_n, rank, features), f32),
        ],
        in_specs=[SMEM, SMEM, whole((parts, 2 * rank, block)), VMEM] + [ANY] * len(ahead),
        out_specs=[ANY] * len(ahead)
        + [
            whole((2 * rank, block)),
            whole((xlo_n * near_n * core_n, rank, features)),
        ],
        input_output_aliases={4 + k: k for k in range(len(ahead))},
        compiler_params=params(),
        name="rank",
    )(place, lengths, back, upstream, *ahead)
    sums += ahead[: len(middle)]
    near_parts = lax.all_to_all(mine, ("xlo", "near", "core"), 0, 0, tiled=True)

    came = leave(ahead[len(middle) :], late)
    ahead = came + [value_parts[k] for k in last]
    *ahead, routed = pl.pallas_call(
        functools.partial(route_kernel, sizes),
        grid=(1,),
        out_shape=parcels * len(ahead) + [struct((far_n, rank, features), bf16)],
        in_specs=[SMEM, SMEM, whole((xlo_n * near_n * core_n, rank, features))]
        + [ANY] * len(ahead),
        out_specs=[ANY] * len(ahead) + [whole((far_n, rank, features))],
        scratch_shapes=[pltpu.VMEM((far_n, rank, features), f32)],
        input_output_aliases={3 + k: k for k in range(len(ahead))},
        compiler_params=params(),
        name="route",
    )(place, tenants, near_parts, *ahead)
    sums += ahead[: len(late)]
    far_parts = lax.all_to_all(routed, "far", 0, 0, tiled=True)
    sums += leave(ahead[len(late) :], last)
    up_grad = pl.pallas_call(
        sum_kernel,
        grid=(1,),
        out_shape=struct((1, rank, features), f32),
        in_specs=[whole((far_n, rank, features))],
        out_specs=whole((1, rank, features)),
        compiler_params=params(),
        name="total",
    )(far_parts)

    gradient = pl.pallas_call(
        gradient_kernel,
        grid=(block // row_step,),
        out_shape=struct((block, width), bf16),
        in_specs=[
            pl.BlockSpec(
                (parts, rows, row_step // rows * features), lambda i: (0, 1, i)
            ),
            pl.BlockSpec((width, values), lambda i: (0, 0)),
            pl.BlockSpec((2 * rank, row_step), lambda i: (0, i)),
            pl.BlockSpec(own.shape, lambda i: (0, 0)),
        ],
        out_specs=pl.BlockSpec((row_step, width), lambda i: (i, 0)),
        compiler_params=params(12),
        cost_estimate=cost(2 * block * width * values, 4 << 20),
        name="gradient",
    )(arrived, base_weight, both, item)
    projected = pl.pallas_call(
        functools.partial(projected_kernel, width),
        grid=(1,),
        out_shape=struct((block, features), bf16),
        in_specs=[whole((2 * rank, block)), whole(own.shape)]
        + [whole((block, features))] * parts,
        out_specs=whole((block, features)),
        compiler_params=params(),
        name="projected",
    )(both, item, *sums)
    return projected, gradient, up_grad


def solution(mesh):
    replicas, parts = mesh.devices.shape
    cores, xlo, near = 2, 2, 4
    sizes = (xlo, replicas // (xlo * near * cores), near, cores)
    fine = Mesh(mesh.devices.reshape(sizes + (parts,)), REP + ("tp",))
    return jax.shard_map(
        functools.partial(on_device, sizes, parts),
        mesh=fine,
        in_specs=(
            P(REP + ("tp",), None),
            P("tp", None),
            P(REP, "tp", None),
            P(REP, None, "tp"),
            P(REP, "tp"),
            P(),
            P(),
        ),
        out_specs=(P(REP, "tp"), P(REP, "tp"), P(REP, None, "tp")),
        check_vma=False,
    )
```

```python
import functools

import jax
import jax.numpy as jnp
from jax import lax
from jax.experimental import pallas as pl
from jax.experimental.pallas import tpu as pltpu
from jax.sharding import Mesh
from jax.sharding import PartitionSpec as P

adapter_scale = 2.0
VMEM = pl.BlockSpec(memory_space=pltpu.VMEM)
SMEM = pl.BlockSpec(memory_space=pltpu.SMEM)
ANY = pl.BlockSpec(memory_space=pl.ANY)
HBM = pl.BlockSpec(memory_space=pltpu.HBM)
REP = ("xlo", "far", "near", "core")


def params(mib=8):
    return pltpu.CompilerParams(vmem_limit_bytes=mib * 1024 * 1024)


def cost(flops, moved):
    return pl.CostEstimate(flops=flops, bytes_accessed=moved, transcendentals=0)


def struct(shape, dtype):
    return jax.ShapeDtypeStruct(shape, dtype)


def whole(shape):
    return pl.BlockSpec(shape, lambda i: (0,) * len(shape))


def dot(a, b, ca, cb):
    return lax.dot_general(
        a, b, (((ca,), (cb,)), ((), ())), preferred_element_type=jnp.float32
    )


def split_place(index, sizes):
    xlo_n, far_n, near_n, core_n = sizes
    core = lax.rem(index, core_n)
    index = lax.div(index, core_n)
    near = lax.rem(index, near_n)
    index = lax.div(index, near_n)
    return lax.div(index, far_n), lax.rem(index, far_n), near, core


def slab_kernel(parts, tokens_ref, upstream_ref, out_ref, slices_ref, fold_ref, sems):
    rows, features = tokens_ref.shape[0], upstream_ref.shape[1]
    width = tokens_ref.shape[1] // parts
    folds = [
        pltpu.make_async_copy(
            upstream_ref.at[pl.ds(g * rows, rows), :],
            fold_ref.at[:, pl.ds(g * features, features)],
            sems.at[1, g],
        )
        for g in range(parts)
    ]
    slices = [
        pltpu.make_async_copy(
            tokens_ref.at[:, pl.ds(s * width, width)], slices_ref.at[s], sems.at[0, s]
        )
        for s in range(parts)
    ]
    for copy in folds + slices:
        copy.start()
    sends = []
    for copy in folds:
        copy.wait()
    for s in range(parts):
        sends.append(
            pltpu.make_async_copy(fold_ref, out_ref.at[s, pl.ds(rows, rows), :], sems.at[2, s])
        )
        sends[-1].start()
    for s in range(parts):
        slices[s].wait()
        sends.append(
            pltpu.make_async_copy(
                slices_ref.at[s], out_ref.at[s, pl.ds(0, rows), :], sems.at[3, s]
            )
        )
        sends[-1].start()
    for copy in sends:
        copy.wait()


def table_kernel(sizes, place_ref, tenants_ref, held_ref, other_ref, out_ref, sems):
    xlo_n, far_n, near_n, core_n = sizes
    _, far, _, core = split_place(place_ref[0], sizes)
    for xlo in range(xlo_n):
        for near in range(near_n):
            block = ((xlo * far_n + far) * near_n + near) * core_n + core
            _, source_far, _, source_core = split_place(tenants_ref[block], sizes)
            slot = xlo * near_n + near

            @pl.when(source_core == core)
            def _():
                pltpu.make_async_copy(
                    held_ref.at[source_far], out_ref.at[slot], sems.at[slot]
                ).start()

            @pl.when(source_core != core)
            def _():
                pltpu.make_async_copy(
                    other_ref.at[source_far], out_ref.at[slot], sems.at[slot]
                ).start()

    for slot in range(xlo_n * near_n):
        pltpu.make_async_copy(held_ref.at[0], out_ref.at[slot], sems.at[slot]).wait()


def value_kernel(columns_ref, weight_ref, *refs):
    outs, mark_ref, held_ref = refs[:-2], refs[-2], refs[-1]
    mark_ref[...] = jnp.zeros_like(mark_ref)
    sources, rows, width = columns_ref.shape
    columns = columns_ref[...].reshape(sources * rows, width)
    held_ref[...] = dot(columns, weight_ref[...], 1, 0).astype(jnp.bfloat16)
    me, parts, features = lax.axis_index("tp"), len(outs), outs[0].shape[1]
    for k, out_ref in enumerate(outs):
        at = pl.multiple_of(lax.rem(me + k, parts) * features, features)
        out_ref[...] = held_ref[:, pl.ds(at, features)]


def low_kernel(
    sizes,
    place_ref,
    tenants_ref,
    offered_ref,
    arrived_ref,
    upstream_ref,
    *refs,
):
    out_ref, item_ref, sem = refs[-3:]
    xlo, _, near, _ = split_place(tenants_ref[place_ref[0]], sizes)
    copy = pltpu.make_async_copy(offered_ref.at[xlo * sizes[2] + near], item_ref, sem)
    copy.start()
    copy.wait()
    sources, rows, width = arrived_ref.shape[0], arrived_ref.shape[1] // 2, arrived_ref.shape[2]
    columns = arrived_ref[:, :rows, :].reshape(sources * rows, width)
    low = dot(item_ref[:, :width], columns, 1, 1)
    back = dot(item_ref[:, width:], upstream_ref[...], 1, 1)
    both = jnp.concatenate([low, back], axis=0).astype(jnp.bfloat16)
    for s in range(out_ref.shape[0]):
        out_ref[s] = both


def rank_kernel(place_ref, lengths_ref, parts_ref, upstream_ref, *refs):
    both_ref, out_ref = refs[-2:]
    length = lengths_ref[place_ref[0]]
    total = parts_ref[0].astype(jnp.float32)
    for s in range(1, parts_ref.shape[0]):
        total = total + parts_ref[s].astype(jnp.float32)
    ranks = both_ref.shape[0]
    total = total.astype(jnp.bfloat16).astype(jnp.float32)
    live = lax.broadcasted_iota(jnp.int32, total.shape, 1) < length
    both = jnp.where(live, adapter_scale * total, 0.0).astype(jnp.bfloat16)
    both_ref[...] = both
    mine = dot(both[: ranks // 2], upstream_ref[...], 1, 0)
    for member in range(out_ref.shape[0]):
        out_ref[member] = mine


def route_kernel(sizes, place_ref, tenants_ref, parts_ref, *refs):
    out_ref, total_ref = refs[-2:]
    xlo_n, far_n, near_n, core_n = sizes
    my_xlo, far, near, my_core = split_place(place_ref[0], sizes)
    total_ref[...] = jnp.zeros_like(total_ref)
    for xlo in range(xlo_n):
        for core in range(core_n):
            block = ((xlo * far_n + far) * near_n + near) * core_n + core
            to_xlo, to_far, to_near, to_core = split_place(tenants_ref[block], sizes)

            @pl.when((to_xlo == my_xlo) & (to_core == my_core))
            def _():
                total_ref[to_far * near_n + to_near] += parts_ref[xlo * core_n + core]

    out_ref[...] = total_ref[...].astype(out_ref.dtype)


def sum_kernel(parts_ref, out_ref):
    total = parts_ref[0].astype(jnp.float32)
    for s in range(1, parts_ref.shape[0]):
        total = total + parts_ref[s].astype(jnp.float32)
    out_ref[0] = total


def projected_kernel(width, both_ref, item_ref, *refs):
    rank, out_ref = item_ref.shape[0], refs[-1]
    total = refs[0][...].astype(jnp.float32)
    for part_ref in refs[1:-1]:
        total = total + part_ref[...].astype(jnp.float32)
    term = dot(both_ref[:rank], item_ref[:, width:], 0, 0)
    out_ref[...] = (total + term).astype(jnp.bfloat16)


def base_kernel(upstream_ref, weight_ref, out_ref, mark_ref):
    mark_ref[...] = jnp.zeros_like(mark_ref)
    sources, _, lanes = upstream_ref.shape
    features = weight_ref.shape[1] // sources
    rows = jnp.concatenate(
        [
            jnp.concatenate(
                [upstream_ref[s, :, at : at + features] for s in range(sources)], axis=1
            )
            for at in range(0, lanes, features)
        ],
        axis=0,
    )
    out_ref[...] = dot(rows, weight_ref[...], 1, 1)


def gradient_kernel(base_ref, both_ref, item_ref, out_ref):
    rank, width = item_ref.shape[0], out_ref.shape[1]
    term = dot(both_ref[rank:], item_ref[:, :width], 0, 0)
    out_ref[...] = (base_ref[...] + term).astype(jnp.bfloat16)


def on_device(
    sizes, parts, tokens, base_weight, adapter_down, adapter_up, upstream, tenants, lengths
):
    bf16, f32 = jnp.bfloat16, jnp.float32
    xlo_n, far_n, near_n, core_n = sizes
    place = lax.axis_index(REP).astype(jnp.int32).reshape(1)
    rows, full_width = tokens.shape
    width = full_width // parts
    block, features = upstream.shape
    rank = adapter_up.shape[1]
    values = base_weight.shape[1]
    row_step, base_step = 128, 256
    mark = struct((8, 128), f32)
    slabs = pl.pallas_call(
        functools.partial(slab_kernel, parts),
        out_shape=struct((parts, 2 * rows, width), bf16),
        in_specs=[HBM, HBM],
        out_specs=HBM,
        scratch_shapes=[
            pltpu.VMEM((parts, rows, width), bf16),
            pltpu.VMEM((rows, width), bf16),
            pltpu.SemaphoreType.DMA((4, parts)),
        ],
        compiler_params=params(60),
        name="slab",
    )(tokens, upstream)
    arrived = lax.all_to_all(slabs, "tp", 0, 0, tiled=True)

    own = jnp.concatenate([adapter_down[0].T, adapter_up[0]], axis=1)
    held = lax.all_gather(own, "far", axis=0, tiled=False)
    other = lax.ppermute(held, "core", [(c, (c + 1) % core_n) for c in range(core_n)])

    *value_parts, value_mark = pl.pallas_call(
        value_kernel,
        grid=(block // row_step,),
        out_shape=[struct((block, features), bf16)] * parts + [mark],
        in_specs=[
            pl.BlockSpec((row_step // rows, rows, width), lambda i: (i, 0, 0)),
            pl.BlockSpec((width, values), lambda i: (0, 0)),
        ],
        out_specs=[pl.BlockSpec((row_step, features), lambda i: (i, 0))] * parts
        + [whole(mark.shape)],
        scratch_shapes=[pltpu.VMEM((row_step, values), bf16)],
        compiler_params=params(12),
        cost_estimate=cost(2 * block * width * values, 4 << 20),
        name="value",
    )(arrived, base_weight)

    table = pl.pallas_call(
        functools.partial(table_kernel, sizes),
        out_shape=struct((xlo_n * near_n,) + own.shape, bf16),
        in_specs=[SMEM, SMEM, ANY, ANY],
        out_specs=ANY,
        scratch_shapes=[pltpu.SemaphoreType.DMA((xlo_n * near_n,))],
        compiler_params=params(),
        name="table",
    )(place, tenants, held, other)
    offered = lax.all_to_all(table, ("xlo", "near"), 0, 0, tiled=True)

    parcel = [struct((block, features), bf16)] * parts
    sent, item = pl.pallas_call(
        functools.partial(low_kernel, sizes),
        grid=(1,),
        out_shape=(struct((parts, 2 * rank, block), bf16), struct(own.shape, bf16)),
        in_specs=[SMEM, SMEM, ANY, VMEM, VMEM, ANY],
        out_specs=(whole((parts, 2 * rank, block)), whole(own.shape)),
        scratch_shapes=[pltpu.SemaphoreType.DMA],
        compiler_params=params(),
        name="low",
    )(place, tenants, offered, arrived, upstream, value_mark)
    back = lax.all_to_all(sent, "tp", 0, 0, tiled=True)

    base, base_mark = pl.pallas_call(
        base_kernel,
        grid=(block // base_step,),
        out_shape=(struct((block, width), f32), mark),
        in_specs=[
            pl.BlockSpec(
                (parts, rows, base_step // rows * features), lambda i: (0, 1, i)
            ),
            pl.BlockSpec((width, values), lambda i: (0, 0)),
        ],
        out_specs=(pl.BlockSpec((base_step, width), lambda i: (i, 0)), whole(mark.shape)),
        compiler_params=params(16),
        cost_estimate=cost(2 * block * width * values, 6 << 20),
        name="base",
    )(arrived, base_weight)
    both, mine = pl.pallas_call(
        rank_kernel,
        grid=(1,),
        out_shape=(
            struct((2 * rank, block), bf16),
            struct((xlo_n * core_n, rank, features), f32),
        ),
        in_specs=[SMEM, SMEM, whole((parts, 2 * rank, block)), VMEM, ANY],
        out_specs=(
            whole((2 * rank, block)),
            whole((xlo_n * core_n, rank, features)),
        ),
        compiler_params=params(),
        name="rank",
    )(place, lengths, back, upstream, base_mark)
    near_parts = lax.all_to_all(mine, ("xlo", "core"), 0, 0, tiled=True)
    *value_parts, routed = pl.pallas_call(
        functools.partial(route_kernel, sizes),
        grid=(1,),
        out_shape=parcel + [struct((far_n * near_n, rank, features), bf16)],
        in_specs=[SMEM, SMEM, whole((xlo_n * core_n, rank, features))] + [ANY] * parts,
        out_specs=[ANY] * parts + [whole((far_n * near_n, rank, features))],
        scratch_shapes=[pltpu.VMEM((far_n * near_n, rank, features), f32)],
        input_output_aliases={3 + k: k for k in range(parts)},
        compiler_params=params(),
        name="route",
    )(place, tenants, near_parts, *value_parts)
    far_parts = lax.all_to_all(routed, ("far", "near"), 0, 0, tiled=True)
    sums = [value_parts[0]] + [
        lax.ppermute(value_parts[k], "tp", [(d, (d + k) % parts) for d in range(parts)])
        for k in range(1, parts)
    ]
    up_grad = pl.pallas_call(
        sum_kernel,
        grid=(1,),
        out_shape=struct((1, rank, features), f32),
        in_specs=[whole((far_n * near_n, rank, features))],
        out_specs=whole((1, rank, features)),
        compiler_params=params(),
        name="total",
    )(far_parts)

    gradient = pl.pallas_call(
        gradient_kernel,
        grid=(block // row_step,),
        out_shape=struct((block, width), bf16),
        in_specs=[
            pl.BlockSpec((row_step, width), lambda i: (i, 0)),
            pl.BlockSpec((2 * rank, row_step), lambda i: (0, i)),
            pl.BlockSpec(own.shape, lambda i: (0, 0)),
        ],
        out_specs=pl.BlockSpec((row_step, width), lambda i: (i, 0)),
        compiler_params=params(),
        cost_estimate=cost(2 * block * width * rank, 3 << 20),
        name="gradient",
    )(base, both, item)
    projected = pl.pallas_call(
        functools.partial(projected_kernel, width),
        grid=(1,),
        out_shape=struct((block, features), bf16),
        in_specs=[whole((2 * rank, block)), whole(own.shape)]
        + [whole((block, features))] * parts,
        out_specs=whole((block, features)),
        compiler_params=params(),
        name="projected",
    )(both, item, *sums)
    return projected, gradient, up_grad


def solution(mesh):
    replicas, parts = mesh.devices.shape
    cores, xlo, near = 2, 2, 4
    sizes = (xlo, replicas // (xlo * near * cores), near, cores)
    fine = Mesh(mesh.devices.reshape(sizes + (parts,)), REP + ("tp",))
    return jax.shard_map(
        functools.partial(on_device, sizes, parts),
        mesh=fine,
        in_specs=(
            P(REP + ("tp",), None),
            P("tp", None),
            P(REP, "tp", None),
            P(REP, None, "tp"),
            P(REP, "tp"),
            P(),
            P(),
        ),
        out_specs=(P(REP, "tp"), P(REP, "tp"), P(REP, None, "tp")),
        check_vma=False,
    )
```

```python
import functools

import jax
import jax.numpy as jnp
from jax import lax
from jax.experimental import pallas as pl
from jax.experimental.pallas import tpu as pltpu
from jax.sharding import Mesh
from jax.sharding import PartitionSpec as P

adapter_scale = 2.0
VMEM = pl.BlockSpec(memory_space=pltpu.VMEM)
SMEM = pl.BlockSpec(memory_space=pltpu.SMEM)
ANY = pl.BlockSpec(memory_space=pl.ANY)
HBM = pl.BlockSpec(memory_space=pltpu.HBM)
REP = ("xlo", "far", "near", "core")


def params(mib=8):
    return pltpu.CompilerParams(vmem_limit_bytes=mib * 1024 * 1024)


def cost(flops, moved):
    return pl.CostEstimate(flops=flops, bytes_accessed=moved, transcendentals=0)


def struct(shape, dtype):
    return jax.ShapeDtypeStruct(shape, dtype)


def whole(shape):
    return pl.BlockSpec(shape, lambda i: (0,) * len(shape))


def dot(a, b, ca, cb):
    return lax.dot_general(
        a, b, (((ca,), (cb,)), ((), ())), preferred_element_type=jnp.float32
    )


def split_place(index, sizes):
    xlo_n, far_n, near_n, core_n = sizes
    core = lax.rem(index, core_n)
    index = lax.div(index, core_n)
    near = lax.rem(index, near_n)
    index = lax.div(index, near_n)
    return lax.div(index, far_n), lax.rem(index, far_n), near, core


def slab_kernel(parts, tokens_ref, upstream_ref, out_ref, slices_ref, fold_ref, sems):
    rows, features = tokens_ref.shape[0], upstream_ref.shape[1]
    width = tokens_ref.shape[1] // parts
    folds = [
        pltpu.make_async_copy(
            upstream_ref.at[pl.ds(g * rows, rows), :],
            fold_ref.at[:, pl.ds(g * features, features)],
            sems.at[1, g],
        )
        for g in range(parts)
    ]
    slices = [
        pltpu.make_async_copy(
            tokens_ref.at[:, pl.ds(s * width, width)], slices_ref.at[s], sems.at[0, s]
        )
        for s in range(parts)
    ]
    for copy in folds + slices:
        copy.start()
    sends = []
    for copy in folds:
        copy.wait()
    for s in range(parts):
        sends.append(
            pltpu.make_async_copy(fold_ref, out_ref.at[s, pl.ds(rows, rows), :], sems.at[2, s])
        )
        sends[-1].start()
    for s in range(parts):
        slices[s].wait()
        sends.append(
            pltpu.make_async_copy(
                slices_ref.at[s], out_ref.at[s, pl.ds(0, rows), :], sems.at[3, s]
            )
        )
        sends[-1].start()
    for copy in sends:
        copy.wait()


def table_kernel(sizes, place_ref, tenants_ref, held_ref, other_ref, out_ref, sems):
    xlo_n, far_n, near_n, core_n = sizes
    _, far, _, core = split_place(place_ref[0], sizes)
    for xlo in range(xlo_n):
        for near in range(near_n):
            block = ((xlo * far_n + far) * near_n + near) * core_n + core
            _, source_far, _, source_core = split_place(tenants_ref[block], sizes)
            slot = xlo * near_n + near

            @pl.when(source_core == core)
            def _():
                pltpu.make_async_copy(
                    held_ref.at[source_far], out_ref.at[slot], sems.at[slot]
                ).start()

            @pl.when(source_core != core)
            def _():
                pltpu.make_async_copy(
                    other_ref.at[source_far], out_ref.at[slot], sems.at[slot]
                ).start()

    for slot in range(xlo_n * near_n):
        pltpu.make_async_copy(held_ref.at[0], out_ref.at[slot], sems.at[slot]).wait()


def unfold(slabs_ref, features):
    sources, _, lanes = slabs_ref.shape
    return jnp.concatenate(
        [
            jnp.concatenate(
                [slabs_ref[s, :, at : at + features] for s in range(sources)], axis=1
            )
            for at in range(0, lanes, features)
        ],
        axis=0,
    )


def value_kernel(columns_ref, weight_ref, *refs):
    outs, mark_ref, held_ref = refs[:-2], refs[-2], refs[-1]
    mark_ref[...] = jnp.zeros_like(mark_ref)
    sources, rows, width = columns_ref.shape
    columns = columns_ref[...].reshape(sources * rows, width)
    held_ref[...] = dot(columns, weight_ref[...], 1, 0).astype(jnp.bfloat16)
    me, parts, features = lax.axis_index("tp"), len(outs), outs[0].shape[1]
    for k, out_ref in enumerate(outs):
        at = pl.multiple_of(lax.rem(me + k, parts) * features, features)
        out_ref[...] = held_ref[:, pl.ds(at, features)]


def base_kernel(upstream_ref, weight_ref, out_ref, mark_ref):
    mark_ref[...] = jnp.zeros_like(mark_ref)
    features = weight_ref.shape[1] // upstream_ref.shape[0]
    out_ref[...] = dot(unfold(upstream_ref, features), weight_ref[...], 1, 1)


def low_kernel(
    sizes,
    parts,
    place_ref,
    tenants_ref,
    lengths_ref,
    offered_ref,
    arrived_ref,
    upstream_ref,
    *refs,
):
    outs, share_ref, item_ref, sem = refs[-3 - parts : -3], *refs[-3:]
    place = place_ref[0]
    xlo, _, near, _ = split_place(tenants_ref[place], sizes)
    copy = pltpu.make_async_copy(offered_ref.at[xlo * sizes[2] + near], item_ref, sem)
    copy.start()
    copy.wait()
    sources, rows, width = arrived_ref.shape[0], arrived_ref.shape[1] // 2, arrived_ref.shape[2]
    columns = arrived_ref[:, :rows, :].reshape(sources * rows, width)
    low = dot(item_ref[:, :width], columns, 1, 1)
    back = dot(item_ref[:, width:], upstream_ref[...], 1, 1)
    both = jnp.concatenate([low, back], axis=0).astype(jnp.bfloat16)
    ranks, lanes = both.shape[0], upstream_ref.shape[1]
    for out_ref in outs:
        for g in range(both.shape[1] // lanes):
            out_ref[g * ranks : (g + 1) * ranks, :] = both[:, g * lanes : (g + 1) * lanes]
    live = lax.broadcasted_iota(jnp.int32, low.shape, 1) < lengths_ref[place]
    low = jnp.where(live, adapter_scale * low, 0.0).astype(jnp.bfloat16)
    share = dot(low, unfold(arrived_ref.at[:, rows:, :], lanes), 1, 0)
    for slot in range(share_ref.shape[0]):
        s = slot % parts
        share_ref[slot] = share[:, s * lanes : (s + 1) * lanes]


def route_kernel(sizes, parts, place_ref, tenants_ref, shares_ref, *refs):
    out_ref = refs[-1]
    xlo_n, far_n, near_n, core_n = sizes
    my_xlo, far, near, my_core = split_place(place_ref[0], sizes)
    sums, slots, mine = [], [], []
    for xlo in range(xlo_n):
        for core in range(core_n):
            block = ((xlo * far_n + far) * near_n + near) * core_n + core
            to_xlo, to_far, to_near, to_core = split_place(tenants_ref[block], sizes)
            first = (xlo * core_n + core) * parts
            total = shares_ref[first]
            for s in range(1, parts):
                total = total + shares_ref[first + s]
            sums.append(total)
            slots.append(to_far * near_n + to_near)
            mine.append((to_xlo == my_xlo) & (to_core == my_core))
    out_ref[...] = jnp.zeros_like(out_ref)
    for slot, wanted in zip(slots, mine):
        total = jnp.zeros_like(sums[0])
        for other, other_slot, other_wanted in zip(sums, slots, mine):
            total = total + jnp.where(other_wanted & (other_slot == slot), other, 0.0)

        @pl.when(wanted)
        def _():
            out_ref[slot] = total.astype(out_ref.dtype)


def sum_kernel(parts_ref, out_ref):
    total = parts_ref[0].astype(jnp.float32)
    for s in range(1, parts_ref.shape[0]):
        total = total + parts_ref[s].astype(jnp.float32)
    out_ref[0] = total


def finish_kernel(parts, place_ref, lengths_ref, base_ref, item_ref, *refs):
    values, ranks = refs[:parts], refs[parts : 2 * parts]
    projected_ref, gradient_ref = refs[2 * parts :]
    total = ranks[0][...].astype(jnp.float32)
    for ref in ranks[1:]:
        total = total + ref[...].astype(jnp.float32)
    total = total.astype(jnp.bfloat16).astype(jnp.float32)
    token = lax.broadcasted_iota(jnp.int32, total.shape, 1) + pl.program_id(0) * total.shape[1]
    live = token < lengths_ref[place_ref[0]]
    both = jnp.where(live, adapter_scale * total, 0.0).astype(jnp.bfloat16)
    rank, width = item_ref.shape[0], gradient_ref.shape[1]
    term = dot(both[rank:], item_ref[:, :width], 0, 0)
    gradient_ref[...] = (base_ref[...] + term).astype(jnp.bfloat16)
    value = values[0][...].astype(jnp.float32)
    for ref in values[1:]:
        value = value + ref[...].astype(jnp.float32)
    term = dot(both[:rank], item_ref[:, width:], 0, 0)
    projected_ref[...] = (value + term).astype(jnp.bfloat16)


def on_device(
    sizes, parts, tokens, base_weight, adapter_down, adapter_up, upstream, tenants, lengths
):
    bf16, f32 = jnp.bfloat16, jnp.float32
    xlo_n, far_n, near_n, core_n = sizes
    place = lax.axis_index(REP).astype(jnp.int32).reshape(1)
    rows, full_width = tokens.shape
    width = full_width // parts
    block, features = upstream.shape
    rank = adapter_up.shape[1]
    values = base_weight.shape[1]
    row_step, base_step = 128, 256
    mark = struct((8, 128), f32)
    rank_rows = 2 * rank * block // features
    parcel = struct((block + rank_rows, features), bf16)
    column = xlo_n * core_n * parts
    slabs = pl.pallas_call(
        functools.partial(slab_kernel, parts),
        out_shape=struct((parts, 2 * rows, width), bf16),
        in_specs=[HBM, HBM],
        out_specs=HBM,
        scratch_shapes=[
            pltpu.VMEM((parts, rows, width), bf16),
            pltpu.VMEM((rows, width), bf16),
            pltpu.SemaphoreType.DMA((4, parts)),
        ],
        compiler_params=params(60),
        name="slab",
    )(tokens, upstream)
    arrived = lax.all_to_all(slabs, "tp", 0, 0, tiled=True)

    own = jnp.concatenate([adapter_down[0].T, adapter_up[0]], axis=1)
    held = lax.all_gather(own, "far", axis=0, tiled=False)
    other = lax.ppermute(held, "core", [(c, (c + 1) % core_n) for c in range(core_n)])

    *parcels, value_mark = pl.pallas_call(
        value_kernel,
        grid=(block // row_step,),
        out_shape=[parcel] * parts + [mark],
        in_specs=[
            pl.BlockSpec((row_step // rows, rows, width), lambda i: (i, 0, 0)),
            pl.BlockSpec((width, values), lambda i: (0, 0)),
        ],
        out_specs=[pl.BlockSpec((row_step, features), lambda i: (i, 0))] * parts
        + [whole(mark.shape)],
        scratch_shapes=[pltpu.VMEM((row_step, values), bf16)],
        compiler_params=params(12),
        cost_estimate=cost(2 * block * width * values, 4 << 20),
        name="value",
    )(arrived, base_weight)

    base, base_mark = pl.pallas_call(
        base_kernel,
        grid=(block // base_step,),
        out_shape=(struct((block, width), f32), mark),
        in_specs=[
            pl.BlockSpec(
                (parts, rows, base_step // rows * features), lambda i: (0, 1, i)
            ),
            pl.BlockSpec((width, values), lambda i: (0, 0)),
        ],
        out_specs=(pl.BlockSpec((base_step, width), lambda i: (i, 0)), whole(mark.shape)),
        compiler_params=params(16),
        cost_estimate=cost(2 * block * width * values, 6 << 20),
        name="base",
    )(arrived, base_weight)

    table = pl.pallas_call(
        functools.partial(table_kernel, sizes),
        out_shape=struct((xlo_n * near_n,) + own.shape, bf16),
        in_specs=[SMEM, SMEM, ANY, ANY],
        out_specs=ANY,
        scratch_shapes=[pltpu.SemaphoreType.DMA((xlo_n * near_n,))],
        compiler_params=params(),
        name="table",
    )(place, tenants, held, other)
    offered = lax.all_to_all(table, ("xlo", "near"), 0, 0, tiled=True)

    *parcels, shares, item = pl.pallas_call(
        functools.partial(low_kernel, sizes, parts),
        grid=(1,),
        out_shape=[parcel] * parts
        + [struct((column, rank, features), f32), struct(own.shape, bf16)],
        in_specs=[SMEM, SMEM, SMEM, ANY, VMEM, VMEM, ANY, ANY] + [ANY] * parts,
        out_specs=[pl.BlockSpec((rank_rows, features), lambda i: (block // rank_rows, 0))]
        * parts
        + [whole((column, rank, features)), whole(own.shape)],
        scratch_shapes=[pltpu.SemaphoreType.DMA],
        input_output_aliases={8 + k: k for k in range(parts)},
        compiler_params=params(12),
        name="low",
    )(place, tenants, lengths, offered, arrived, upstream, value_mark, base_mark, *parcels)
    arrived_shares = lax.all_to_all(shares, ("xlo", "core", "tp"), 0, 0, tiled=True)

    def leave(k):
        return lax.ppermute(parcels[k], "tp", [(d, (d + k) % parts) for d in range(parts)])

    early = 1
    for k in range(1, 1 + early):
        parcels[k] = leave(k)
    *parcels, routed = pl.pallas_call(
        functools.partial(route_kernel, sizes, parts),
        grid=(1,),
        out_shape=[parcel] * parts + [struct((far_n * near_n, rank, features), bf16)],
        in_specs=[SMEM, SMEM, whole((column, rank, features))] + [ANY] * parts,
        out_specs=[ANY] * parts + [whole((far_n * near_n, rank, features))],
        input_output_aliases={3 + k: k for k in range(parts)},
        compiler_params=params(),
        name="route",
    )(place, tenants, arrived_shares, *parcels)
    far_parts = lax.all_to_all(routed, ("far", "near"), 0, 0, tiled=True)
    for k in range(1 + early, parts):
        parcels[k] = leave(k)
    up_grad = pl.pallas_call(
        sum_kernel,
        grid=(1,),
        out_shape=struct((1, rank, features), f32),
        in_specs=[whole((far_n * near_n, rank, features))],
        out_specs=whole((1, rank, features)),
        compiler_params=params(),
        name="total",
    )(far_parts)

    group = 2 * rank
    projected, gradient = pl.pallas_call(
        functools.partial(finish_kernel, parts),
        grid=(block // features,),
        out_shape=(struct((block, features), bf16), struct((block, width), bf16)),
        in_specs=[
            SMEM,
            SMEM,
            pl.BlockSpec((features, width), lambda i: (i, 0)),
            pl.BlockSpec(own.shape, lambda i: (0, 0)),
        ]
        + [pl.BlockSpec((features, features), lambda i: (i, 0))] * parts
        + [pl.BlockSpec((group, features), lambda i: (block // group + i, 0))] * parts,
        out_specs=(
            pl.BlockSpec((features, features), lambda i: (i, 0)),
            pl.BlockSpec((features, width), lambda i: (i, 0)),
        ),
        compiler_params=params(),
        cost_estimate=cost(2 * block * width * rank, 5 << 20),
        name="finish",
    )(place, lengths, base, item, *parcels, *parcels)
    return projected, gradient, up_grad


def solution(mesh):
    replicas, parts = mesh.devices.shape
    cores, xlo, near = 2, 2, 4
    sizes = (xlo, replicas // (xlo * near * cores), near, cores)
    fine = Mesh(mesh.devices.reshape(sizes + (parts,)), REP + ("tp",))
    return jax.shard_map(
        functools.partial(on_device, sizes, parts),
        mesh=fine,
        in_specs=(
            P(REP + ("tp",), None),
            P("tp", None),
            P(REP, "tp", None),
            P(REP, None, "tp"),
            P(REP, "tp"),
            P(),
            P(),
        ),
        out_specs=(P(REP, "tp"), P(REP, "tp"), P(REP, None, "tp")),
        check_vma=False,
    )
```

```python
import functools

import jax
import jax.numpy as jnp
from jax import lax
from jax.experimental import pallas as pl
from jax.experimental.pallas import tpu as pltpu
from jax.sharding import Mesh
from jax.sharding import PartitionSpec as P

adapter_scale = 2.0
VMEM = pl.BlockSpec(memory_space=pltpu.VMEM)
SMEM = pl.BlockSpec(memory_space=pltpu.SMEM)
ANY = pl.BlockSpec(memory_space=pl.ANY)
HBM = pl.BlockSpec(memory_space=pltpu.HBM)
REP = ("xlo", "far", "near", "core")


def params(mib=8):
    return pltpu.CompilerParams(vmem_limit_bytes=mib * 1024 * 1024)


def cost(flops, moved):
    return pl.CostEstimate(flops=flops, bytes_accessed=moved, transcendentals=0)


def struct(shape, dtype):
    return jax.ShapeDtypeStruct(shape, dtype)


def whole(shape):
    return pl.BlockSpec(shape, lambda i: (0,) * len(shape))


def dot(a, b, ca, cb):
    return lax.dot_general(
        a, b, (((ca,), (cb,)), ((), ())), preferred_element_type=jnp.float32
    )


def split_place(index, sizes):
    xlo_n, far_n, near_n, core_n = sizes
    core = lax.rem(index, core_n)
    index = lax.div(index, core_n)
    near = lax.rem(index, near_n)
    index = lax.div(index, near_n)
    return lax.div(index, far_n), lax.rem(index, far_n), near, core


def slab_kernel(parts, tokens_ref, upstream_ref, out_ref, slices_ref, fold_ref, sems):
    rows, features = tokens_ref.shape[0], upstream_ref.shape[1]
    width = tokens_ref.shape[1] // parts
    folds = [
        pltpu.make_async_copy(
            upstream_ref.at[pl.ds(g * rows, rows), :],
            fold_ref.at[:, pl.ds(g * features, features)],
            sems.at[1, g],
        )
        for g in range(parts)
    ]
    slices = [
        pltpu.make_async_copy(
            tokens_ref.at[:, pl.ds(s * width, width)], slices_ref.at[s], sems.at[0, s]
        )
        for s in range(parts)
    ]
    for copy in folds + slices:
        copy.start()
    sends = []
    for copy in folds:
        copy.wait()
    for s in range(parts):
        sends.append(
            pltpu.make_async_copy(fold_ref, out_ref.at[s, pl.ds(rows, rows), :], sems.at[2, s])
        )
        sends[-1].start()
    for s in range(parts):
        slices[s].wait()
        sends.append(
            pltpu.make_async_copy(
                slices_ref.at[s], out_ref.at[s, pl.ds(0, rows), :], sems.at[3, s]
            )
        )
        sends[-1].start()
    for copy in sends:
        copy.wait()


def table_kernel(sizes, place_ref, tenants_ref, held_ref, other_ref, out_ref, sems):
    xlo_n, far_n, near_n, core_n = sizes
    _, far, _, core = split_place(place_ref[0], sizes)
    for xlo in range(xlo_n):
        for near in range(near_n):
            block = ((xlo * far_n + far) * near_n + near) * core_n + core
            _, source_far, _, source_core = split_place(tenants_ref[block], sizes)
            slot = xlo * near_n + near

            @pl.when(source_core == core)
            def _():
                pltpu.make_async_copy(
                    held_ref.at[source_far], out_ref.at[slot], sems.at[slot]
                ).start()

            @pl.when(source_core != core)
            def _():
                pltpu.make_async_copy(
                    other_ref.at[source_far], out_ref.at[slot], sems.at[slot]
                ).start()

    for slot in range(xlo_n * near_n):
        pltpu.make_async_copy(held_ref.at[0], out_ref.at[slot], sems.at[slot]).wait()


def unfold(slabs_ref, features):
    sources, _, lanes = slabs_ref.shape
    return jnp.concatenate(
        [
            jnp.concatenate(
                [slabs_ref[s, :, at : at + features] for s in range(sources)], axis=1
            )
            for at in range(0, lanes, features)
        ],
        axis=0,
    )


def value_kernel(partners, columns_ref, weight_ref, *refs):
    outs, mark_ref, held_ref = refs[:-2], refs[-2], refs[-1]
    mark_ref[...] = jnp.zeros_like(mark_ref)
    sources, rows, width = columns_ref.shape
    columns = columns_ref[...].reshape(sources * rows, width)
    held_ref[...] = dot(columns, weight_ref[...], 1, 0).astype(jnp.bfloat16)
    me, features = lax.axis_index("tp"), outs[0].shape[1]
    for k, out_ref in zip(partners, outs):
        at = pl.multiple_of(jnp.bitwise_xor(me, k) * features, features)
        out_ref[...] = held_ref[:, pl.ds(at, features)]


def base_kernel(upstream_ref, weight_ref, out_ref, mark_ref):
    mark_ref[...] = jnp.zeros_like(mark_ref)
    features = weight_ref.shape[1] // upstream_ref.shape[0]
    out_ref[...] = dot(unfold(upstream_ref, features), weight_ref[...], 1, 1)


def low_kernel(
    sizes,
    parts,
    place_ref,
    tenants_ref,
    lengths_ref,
    offered_ref,
    arrived_ref,
    upstream_ref,
    *refs,
):
    outs, share_ref, item_ref, sem = refs[-3 - parts : -3], *refs[-3:]
    place = place_ref[0]
    xlo, _, near, _ = split_place(tenants_ref[place], sizes)
    copy = pltpu.make_async_copy(offered_ref.at[xlo * sizes[2] + near], item_ref, sem)
    copy.start()
    copy.wait()
    sources, rows, width = arrived_ref.shape[0], arrived_ref.shape[1] // 2, arrived_ref.shape[2]
    columns = arrived_ref[:, :rows, :].reshape(sources * rows, width)
    low = dot(item_ref[:, :width], columns, 1, 1)
    back = dot(item_ref[:, width:], upstream_ref[...], 1, 1)
    both = jnp.concatenate([low, back], axis=0).astype(jnp.bfloat16)
    ranks, lanes = both.shape[0], upstream_ref.shape[1]
    for out_ref in outs:
        for g in range(both.shape[1] // lanes):
            out_ref[g * ranks : (g + 1) * ranks, :] = both[:, g * lanes : (g + 1) * lanes]
    live = lax.broadcasted_iota(jnp.int32, low.shape, 1) < lengths_ref[place]
    low = jnp.where(live, adapter_scale * low, 0.0).astype(jnp.bfloat16)
    share = dot(low, unfold(arrived_ref.at[:, rows:, :], lanes), 1, 0)
    for slot in range(share_ref.shape[0]):
        s = slot % parts
        share_ref[slot] = share[:, s * lanes : (s + 1) * lanes].astype(share_ref.dtype)


def route_kernel(sizes, parts, place_ref, tenants_ref, shares_ref, *refs):
    out_ref = refs[-1]
    xlo_n, far_n, near_n, core_n = sizes
    my_xlo, far, near, my_core = split_place(place_ref[0], sizes)
    sums, slots, mine = [], [], []
    for xlo in range(xlo_n):
        for core in range(core_n):
            block = ((xlo * far_n + far) * near_n + near) * core_n + core
            to_xlo, to_far, to_near, to_core = split_place(tenants_ref[block], sizes)
            first = (xlo * core_n + core) * parts
            total = shares_ref[first].astype(jnp.float32)
            for s in range(1, parts):
                total = total + shares_ref[first + s].astype(jnp.float32)
            sums.append(total)
            slots.append(to_far * near_n + to_near)
            mine.append((to_xlo == my_xlo) & (to_core == my_core))
    out_ref[...] = jnp.zeros_like(out_ref)
    for slot, wanted in zip(slots, mine):
        total = jnp.zeros_like(sums[0])
        for other, other_slot, other_wanted in zip(sums, slots, mine):
            total = total + jnp.where(other_wanted & (other_slot == slot), other, 0.0)

        @pl.when(wanted)
        def _():
            out_ref[slot] = total.astype(out_ref.dtype)


def sum_kernel(parts_ref, out_ref):
    total = parts_ref[0].astype(jnp.float32)
    for s in range(1, parts_ref.shape[0]):
        total = total + parts_ref[s].astype(jnp.float32)
    out_ref[0] = total


def finish_kernel(parts, place_ref, lengths_ref, base_ref, item_ref, *refs):
    values, ranks = refs[:parts], refs[parts : 2 * parts]
    projected_ref, gradient_ref = refs[2 * parts :]
    total = ranks[0][...].astype(jnp.float32)
    for ref in ranks[1:]:
        total = total + ref[...].astype(jnp.float32)
    total = total.astype(jnp.bfloat16).astype(jnp.float32)
    token = lax.broadcasted_iota(jnp.int32, total.shape, 1) + pl.program_id(0) * total.shape[1]
    live = token < lengths_ref[place_ref[0]]
    both = jnp.where(live, adapter_scale * total, 0.0).astype(jnp.bfloat16)
    rank, width = item_ref.shape[0], gradient_ref.shape[1]
    term = dot(both[rank:], item_ref[:, :width], 0, 0)
    gradient_ref[...] = (base_ref[...] + term).astype(jnp.bfloat16)
    value = values[0][...].astype(jnp.float32)
    for ref in values[1:]:
        value = value + ref[...].astype(jnp.float32)
    term = dot(both[:rank], item_ref[:, width:], 0, 0)
    projected_ref[...] = (value + term).astype(jnp.bfloat16)


def on_device(
    sizes, parts, tokens, base_weight, adapter_down, adapter_up, upstream, tenants, lengths
):
    bf16, f32 = jnp.bfloat16, jnp.float32
    xlo_n, far_n, near_n, core_n = sizes
    place = lax.axis_index(REP).astype(jnp.int32).reshape(1)
    rows, full_width = tokens.shape
    width = full_width // parts
    block, features = upstream.shape
    rank = adapter_up.shape[1]
    values = base_weight.shape[1]
    row_step, base_step = 128, 256
    mark = struct((8, 128), f32)
    rank_rows = 2 * rank * block // features
    parcel = struct((block + rank_rows, features), bf16)
    column = xlo_n * core_n * parts
    partners = [0] + sorted(
        range(1, parts), key=lambda k: -(2 * (k % 2) + (0, 1, 2, 1)[k // 2 % 4])
    )
    slabs = pl.pallas_call(
        functools.partial(slab_kernel, parts),
        out_shape=struct((parts, 2 * rows, width), bf16),
        in_specs=[HBM, HBM],
        out_specs=HBM,
        scratch_shapes=[
            pltpu.VMEM((parts, rows, width), bf16),
            pltpu.VMEM((rows, width), bf16),
            pltpu.SemaphoreType.DMA((4, parts)),
        ],
        compiler_params=params(60),
        name="slab",
    )(tokens, upstream)
    arrived = lax.all_to_all(slabs, "tp", 0, 0, tiled=True)

    own = jnp.concatenate([adapter_down[0].T, adapter_up[0]], axis=1)
    held = lax.all_gather(own, "far", axis=0, tiled=False)
    other = lax.ppermute(held, "core", [(c, (c + 1) % core_n) for c in range(core_n)])

    *parcels, value_mark = pl.pallas_call(
        functools.partial(value_kernel, partners),
        grid=(block // row_step,),
        out_shape=[parcel] * parts + [mark],
        in_specs=[
            pl.BlockSpec((row_step // rows, rows, width), lambda i: (i, 0, 0)),
            pl.BlockSpec((width, values), lambda i: (0, 0)),
        ],
        out_specs=[pl.BlockSpec((row_step, features), lambda i: (i, 0))] * parts
        + [whole(mark.shape)],
        scratch_shapes=[pltpu.VMEM((row_step, values), bf16)],
        compiler_params=params(12),
        cost_estimate=cost(2 * block * width * values, 4 << 20),
        name="value",
    )(arrived, base_weight)

    base, base_mark = pl.pallas_call(
        base_kernel,
        grid=(block // base_step,),
        out_shape=(struct((block, width), f32), mark),
        in_specs=[
            pl.BlockSpec(
                (parts, rows, base_step // rows * features), lambda i: (0, 1, i)
            ),
            pl.BlockSpec((width, values), lambda i: (0, 0)),
        ],
        out_specs=(pl.BlockSpec((base_step, width), lambda i: (i, 0)), whole(mark.shape)),
        compiler_params=params(16),
        cost_estimate=cost(2 * block * width * values, 6 << 20),
        name="base",
    )(arrived, base_weight)

    table = pl.pallas_call(
        functools.partial(table_kernel, sizes),
        out_shape=struct((xlo_n * near_n,) + own.shape, bf16),
        in_specs=[SMEM, SMEM, ANY, ANY],
        out_specs=ANY,
        scratch_shapes=[pltpu.SemaphoreType.DMA((xlo_n * near_n,))],
        compiler_params=params(),
        name="table",
    )(place, tenants, held, other)
    offered = lax.all_to_all(table, ("xlo", "near"), 0, 0, tiled=True)

    *parcels, shares, item = pl.pallas_call(
        functools.partial(low_kernel, sizes, parts),
        grid=(1,),
        out_shape=[parcel] * parts
        + [struct((column, rank, features), bf16), struct(own.shape, bf16)],
        in_specs=[SMEM, SMEM, SMEM, ANY, VMEM, VMEM, ANY, ANY] + [ANY] * parts,
        out_specs=[pl.BlockSpec((rank_rows, features), lambda i: (block // rank_rows, 0))]
        * parts
        + [whole((column, rank, features)), whole(own.shape)],
        scratch_shapes=[pltpu.SemaphoreType.DMA],
        input_output_aliases={8 + k: k for k in range(parts)},
        compiler_params=params(12),
        name="low",
    )(place, tenants, lengths, offered, arrived, upstream, value_mark, base_mark, *parcels)
    arrived_shares = lax.all_to_all(shares, ("xlo", "core", "tp"), 0, 0, tiled=True)

    *parcels, routed = pl.pallas_call(
        functools.partial(route_kernel, sizes, parts),
        grid=(1,),
        out_shape=[parcel] * parts + [struct((far_n * near_n, rank, features), bf16)],
        in_specs=[SMEM, SMEM, whole((column, rank, features))] + [ANY] * parts,
        out_specs=[ANY] * parts + [whole((far_n * near_n, rank, features))],
        input_output_aliases={3 + k: k for k in range(parts)},
        compiler_params=params(),
        name="route",
    )(place, tenants, arrived_shares, *parcels)
    far_parts = lax.all_to_all(routed, ("far", "near"), 0, 0, tiled=True)
    parcels = parcels[:1] + [
        lax.ppermute(parcel, "tp", [(d, d ^ k) for d in range(parts)])
        for k, parcel in zip(partners[1:], parcels[1:])
    ]
    up_grad = pl.pallas_call(
        sum_kernel,
        grid=(1,),
        out_shape=struct((1, rank, features), f32),
        in_specs=[whole((far_n * near_n, rank, features))],
        out_specs=whole((1, rank, features)),
        compiler_params=params(),
        name="total",
    )(far_parts)

    group = 2 * rank
    projected, gradient = pl.pallas_call(
        functools.partial(finish_kernel, parts),
        grid=(block // features,),
        out_shape=(struct((block, features), bf16), struct((block, width), bf16)),
        in_specs=[
            SMEM,
            SMEM,
            pl.BlockSpec((features, width), lambda i: (i, 0)),
            pl.BlockSpec(own.shape, lambda i: (0, 0)),
        ]
        + [pl.BlockSpec((features, features), lambda i: (i, 0))] * parts
        + [pl.BlockSpec((group, features), lambda i: (block // group + i, 0))] * parts,
        out_specs=(
            pl.BlockSpec((features, features), lambda i: (i, 0)),
            pl.BlockSpec((features, width), lambda i: (i, 0)),
        ),
        compiler_params=params(),
        cost_estimate=cost(2 * block * width * rank, 5 << 20),
        name="finish",
    )(place, lengths, base, item, *parcels, *parcels)
    return projected, gradient, up_grad


def solution(mesh):
    replicas, parts = mesh.devices.shape
    cores, xlo, near = 2, 2, 4
    sizes = (xlo, replicas // (xlo * near * cores), near, cores)
    fine = Mesh(mesh.devices.reshape(sizes + (parts,)), REP + ("tp",))
    return jax.shard_map(
        functools.partial(on_device, sizes, parts),
        mesh=fine,
        in_specs=(
            P(REP + ("tp",), None),
            P("tp", None),
            P(REP, "tp", None),
            P(REP, None, "tp"),
            P(REP, "tp"),
            P(),
            P(),
        ),
        out_specs=(P(REP, "tp"), P(REP, "tp"), P(REP, None, "tp")),
        check_vma=False,
    )
```

```python
import functools

import jax
import jax.numpy as jnp
from jax import lax
from jax.experimental import pallas as pl
from jax.experimental.pallas import tpu as pltpu
from jax.sharding import Mesh
from jax.sharding import PartitionSpec as P

adapter_scale = 2.0
VMEM = pl.BlockSpec(memory_space=pltpu.VMEM)
SMEM = pl.BlockSpec(memory_space=pltpu.SMEM)
ANY = pl.BlockSpec(memory_space=pl.ANY)
HBM = pl.BlockSpec(memory_space=pltpu.HBM)
REP = ("xlo", "far", "near", "core")


def params(mib=8):
    return pltpu.CompilerParams(vmem_limit_bytes=mib * 1024 * 1024)


def cost(flops, moved):
    return pl.CostEstimate(flops=flops, bytes_accessed=moved, transcendentals=0)


def struct(shape, dtype):
    return jax.ShapeDtypeStruct(shape, dtype)


def whole(shape):
    return pl.BlockSpec(shape, lambda i: (0,) * len(shape))


def dot(a, b, ca, cb):
    return lax.dot_general(
        a, b, (((ca,), (cb,)), ((), ())), preferred_element_type=jnp.float32
    )


def split_place(index, sizes):
    xlo_n, far_n, near_n, core_n = sizes
    core = lax.rem(index, core_n)
    index = lax.div(index, core_n)
    near = lax.rem(index, near_n)
    index = lax.div(index, near_n)
    return lax.div(index, far_n), lax.rem(index, far_n), near, core


def slab_kernel(parts, tokens_ref, upstream_ref, out_ref, slices_ref, fold_ref, sems):
    rows, features = tokens_ref.shape[0], upstream_ref.shape[1]
    width = tokens_ref.shape[1] // parts
    folds = [
        pltpu.make_async_copy(
            upstream_ref.at[pl.ds(g * rows, rows), :],
            fold_ref.at[:, pl.ds(g * features, features)],
            sems.at[1, g],
        )
        for g in range(parts)
    ]
    slices = [
        pltpu.make_async_copy(
            tokens_ref.at[:, pl.ds(s * width, width)], slices_ref.at[s], sems.at[0, s]
        )
        for s in range(parts)
    ]
    for copy in folds + slices:
        copy.start()
    sends = []
    for copy in folds:
        copy.wait()
    for s in range(parts):
        sends.append(
            pltpu.make_async_copy(fold_ref, out_ref.at[s, pl.ds(rows, rows), :], sems.at[2, s])
        )
        sends[-1].start()
    for s in range(parts):
        slices[s].wait()
        sends.append(
            pltpu.make_async_copy(
                slices_ref.at[s], out_ref.at[s, pl.ds(0, rows), :], sems.at[3, s]
            )
        )
        sends[-1].start()
    for copy in sends:
        copy.wait()


def table_kernel(sizes, place_ref, tenants_ref, held_ref, other_ref, out_ref, sems):
    xlo_n, far_n, near_n, core_n = sizes
    _, far, _, core = split_place(place_ref[0], sizes)
    for xlo in range(xlo_n):
        for near in range(near_n):
            block = ((xlo * far_n + far) * near_n + near) * core_n + core
            _, source_far, _, source_core = split_place(tenants_ref[block], sizes)
            slot = xlo * near_n + near

            @pl.when(source_core == core)
            def _():
                pltpu.make_async_copy(
                    held_ref.at[source_far], out_ref.at[slot], sems.at[slot]
                ).start()

            @pl.when(source_core != core)
            def _():
                pltpu.make_async_copy(
                    other_ref.at[source_far], out_ref.at[slot], sems.at[slot]
                ).start()

    for slot in range(xlo_n * near_n):
        pltpu.make_async_copy(held_ref.at[0], out_ref.at[slot], sems.at[slot]).wait()


def unfold(slabs_ref, features):
    sources, _, lanes = slabs_ref.shape
    return jnp.concatenate(
        [
            jnp.concatenate(
                [slabs_ref[s, :, at : at + features] for s in range(sources)], axis=1
            )
            for at in range(0, lanes, features)
        ],
        axis=0,
    )


def value_kernel(partners, columns_ref, weight_ref, *refs):
    outs, mark_ref, held_ref = refs[:-2], refs[-2], refs[-1]
    mark_ref[...] = jnp.zeros_like(mark_ref)
    sources, rows, width = columns_ref.shape
    columns = columns_ref[...].reshape(sources * rows, width)
    held_ref[...] = dot(columns, weight_ref[...], 1, 0).astype(jnp.bfloat16)
    me, features = lax.axis_index("tp"), outs[0].shape[1]
    for k, out_ref in zip(partners, outs):
        at = pl.multiple_of(jnp.bitwise_xor(me, k) * features, features)
        out_ref[...] = held_ref[:, pl.ds(at, features)]


def base_kernel(upstream_ref, weight_ref, out_ref, mark_ref):
    mark_ref[...] = jnp.zeros_like(mark_ref)
    features = weight_ref.shape[1] // upstream_ref.shape[0]
    out_ref[...] = dot(unfold(upstream_ref, features), weight_ref[...], 1, 1)


def low_kernel(
    sizes,
    parts,
    place_ref,
    tenants_ref,
    lengths_ref,
    offered_ref,
    arrived_ref,
    upstream_ref,
    *refs,
):
    outs, share_ref, item_ref, sem = refs[-3 - parts : -3], *refs[-3:]
    place = place_ref[0]
    xlo, _, near, _ = split_place(tenants_ref[place], sizes)
    copy = pltpu.make_async_copy(offered_ref.at[xlo * sizes[2] + near], item_ref, sem)
    copy.start()
    copy.wait()
    sources, rows, width = arrived_ref.shape[0], arrived_ref.shape[1] // 2, arrived_ref.shape[2]
    columns = arrived_ref[:, :rows, :].reshape(sources * rows, width)
    low = dot(item_ref[:, :width], columns, 1, 1)
    back = dot(item_ref[:, width:], upstream_ref[...], 1, 1)
    both = jnp.concatenate([low, back], axis=0).astype(jnp.bfloat16)
    ranks, lanes = both.shape[0], upstream_ref.shape[1]
    for out_ref in outs:
        for g in range(both.shape[1] // lanes):
            out_ref[g * ranks : (g + 1) * ranks, :] = both[:, g * lanes : (g + 1) * lanes]
    live = lax.broadcasted_iota(jnp.int32, low.shape, 1) < lengths_ref[place]
    low = jnp.where(live, adapter_scale * low, 0.0).astype(jnp.bfloat16)
    share = dot(low, unfold(arrived_ref.at[:, rows:, :], lanes), 1, 0)
    for slot in range(share_ref.shape[0]):
        s = slot % parts
        share_ref[slot] = share[:, s * lanes : (s + 1) * lanes].astype(share_ref.dtype)


def route_kernel(sizes, parts, place_ref, tenants_ref, shares_ref, *refs):
    out_ref = refs[-1]
    xlo_n, far_n, near_n, core_n = sizes
    my_xlo, far, near, my_core = split_place(place_ref[0], sizes)
    sums, slots, mine = [], [], []
    for xlo in range(xlo_n):
        for core in range(core_n):
            block = ((xlo * far_n + far) * near_n + near) * core_n + core
            to_xlo, to_far, to_near, to_core = split_place(tenants_ref[block], sizes)
            first = (xlo * core_n + core) * parts
            total = shares_ref[first].astype(jnp.float32)
            for s in range(1, parts):
                total = total + shares_ref[first + s].astype(jnp.float32)
            sums.append(total)
            slots.append(to_far * near_n + to_near)
            mine.append((to_xlo == my_xlo) & (to_core == my_core))
    out_ref[...] = jnp.zeros_like(out_ref)
    for slot, wanted in zip(slots, mine):
        total = jnp.zeros_like(sums[0])
        for other, other_slot, other_wanted in zip(sums, slots, mine):
            total = total + jnp.where(other_wanted & (other_slot == slot), other, 0.0)

        @pl.when(wanted)
        def _():
            out_ref[slot] = total.astype(out_ref.dtype)


def sum_kernel(parts_ref, out_ref):
    total = parts_ref[0].astype(jnp.float32)
    for s in range(1, parts_ref.shape[0]):
        total = total + parts_ref[s].astype(jnp.float32)
    out_ref[0] = total


def finish_kernel(parts, place_ref, lengths_ref, base_ref, item_ref, *refs):
    values, ranks = refs[:parts], refs[parts : 2 * parts]
    projected_ref, gradient_ref = refs[2 * parts :]
    total = ranks[0][...].astype(jnp.float32)
    for ref in ranks[1:]:
        total = total + ref[...].astype(jnp.float32)
    total = total.astype(jnp.bfloat16).astype(jnp.float32)
    token = lax.broadcasted_iota(jnp.int32, total.shape, 1) + pl.program_id(0) * total.shape[1]
    live = token < lengths_ref[place_ref[0]]
    both = jnp.where(live, adapter_scale * total, 0.0).astype(jnp.bfloat16)
    rank, width = item_ref.shape[0], gradient_ref.shape[1]
    term = dot(both[rank:], item_ref[:, :width], 0, 0)
    gradient_ref[...] = (base_ref[...] + term).astype(jnp.bfloat16)
    value = values[0][...].astype(jnp.float32)
    for ref in values[1:]:
        value = value + ref[...].astype(jnp.float32)
    term = dot(both[:rank], item_ref[:, width:], 0, 0)
    projected_ref[...] = (value + term).astype(jnp.bfloat16)


def on_device(
    sizes, parts, tokens, base_weight, adapter_down, adapter_up, upstream, tenants, lengths
):
    bf16, f32 = jnp.bfloat16, jnp.float32
    xlo_n, far_n, near_n, core_n = sizes
    place = lax.axis_index(REP).astype(jnp.int32).reshape(1)
    rows, full_width = tokens.shape
    width = full_width // parts
    block, features = upstream.shape
    rank = adapter_up.shape[1]
    values = base_weight.shape[1]
    row_step, base_step = 128, 256
    mark = struct((8, 128), f32)
    rank_rows = 2 * rank * block // features
    parcel = struct((block + rank_rows, features), bf16)
    column = xlo_n * core_n * parts
    partners = [0] + sorted(
        range(1, parts), key=lambda k: -(2 * (k % 2) + (0, 1, 2, 1)[k // 2 % 4])
    )
    slabs = pl.pallas_call(
        functools.partial(slab_kernel, parts),
        out_shape=struct((parts, 2 * rows, width), bf16),
        in_specs=[HBM, HBM],
        out_specs=HBM,
        scratch_shapes=[
            pltpu.VMEM((parts, rows, width), bf16),
            pltpu.VMEM((rows, width), bf16),
            pltpu.SemaphoreType.DMA((4, parts)),
        ],
        compiler_params=params(60),
        name="slab",
    )(tokens, upstream)
    arrived = lax.all_to_all(slabs, "tp", 0, 0, tiled=True)

    own = jnp.concatenate([adapter_down[0].T, adapter_up[0]], axis=1)
    held = lax.all_gather(own, "far", axis=0, tiled=False)
    other = lax.ppermute(held, "core", [(c, (c + 1) % core_n) for c in range(core_n)])

    *parcels, value_mark = pl.pallas_call(
        functools.partial(value_kernel, partners),
        grid=(block // row_step,),
        out_shape=[parcel] * parts + [mark],
        in_specs=[
            pl.BlockSpec((row_step // rows, rows, width), lambda i: (i, 0, 0)),
            pl.BlockSpec((width, values), lambda i: (0, 0)),
        ],
        out_specs=[pl.BlockSpec((row_step, features), lambda i: (i, 0))] * parts
        + [whole(mark.shape)],
        scratch_shapes=[pltpu.VMEM((row_step, values), bf16)],
        compiler_params=params(12),
        cost_estimate=cost(2 * block * width * values, 4 << 20),
        name="value",
    )(arrived, base_weight)

    base, base_mark = pl.pallas_call(
        base_kernel,
        grid=(block // base_step,),
        out_shape=(struct((block, width), f32), mark),
        in_specs=[
            pl.BlockSpec(
                (parts, rows, base_step // rows * features), lambda i: (0, 1, i)
            ),
            pl.BlockSpec((width, values), lambda i: (0, 0)),
        ],
        out_specs=(pl.BlockSpec((base_step, width), lambda i: (i, 0)), whole(mark.shape)),
        compiler_params=params(16),
        cost_estimate=cost(2 * block * width * values, 6 << 20),
        name="base",
    )(arrived, base_weight)

    table = pl.pallas_call(
        functools.partial(table_kernel, sizes),
        out_shape=struct((xlo_n * near_n,) + own.shape, bf16),
        in_specs=[SMEM, SMEM, ANY, ANY],
        out_specs=ANY,
        scratch_shapes=[pltpu.SemaphoreType.DMA((xlo_n * near_n,))],
        compiler_params=params(),
        name="table",
    )(place, tenants, held, other)
    offered = lax.all_to_all(table, ("xlo", "near"), 0, 0, tiled=True)

    *parcels, shares, item = pl.pallas_call(
        functools.partial(low_kernel, sizes, parts),
        grid=(1,),
        out_shape=[parcel] * parts
        + [struct((column, rank, features), bf16), struct(own.shape, bf16)],
        in_specs=[SMEM, SMEM, SMEM, ANY, VMEM, VMEM, ANY, ANY] + [ANY] * parts,
        out_specs=[pl.BlockSpec((rank_rows, features), lambda i: (block // rank_rows, 0))]
        * parts
        + [whole((column, rank, features)), whole(own.shape)],
        scratch_shapes=[pltpu.SemaphoreType.DMA],
        input_output_aliases={8 + k: k for k in range(parts)},
        compiler_params=params(12),
        name="low",
    )(place, tenants, lengths, offered, arrived, upstream, value_mark, base_mark, *parcels)
    arrived_shares = lax.all_to_all(shares, ("xlo", "core", "tp"), 0, 0, tiled=True)

    *parcels, routed = pl.pallas_call(
        functools.partial(route_kernel, sizes, parts),
        grid=(1,),
        out_shape=[parcel] * parts + [struct((far_n * near_n, rank, features), bf16)],
        in_specs=[SMEM, SMEM, whole((column, rank, features))] + [ANY] * parts,
        out_specs=[ANY] * parts + [whole((far_n * near_n, rank, features))],
        input_output_aliases={3 + k: k for k in range(parts)},
        compiler_params=params(),
        name="route",
    )(place, tenants, arrived_shares, *parcels)
    far_parts = lax.all_to_all(routed, ("far", "near"), 0, 0, tiled=True)
    parcels = parcels[:1] + [
        lax.ppermute(parcel, "tp", [(d, d ^ k) for d in range(parts)])
        for k, parcel in zip(partners[1:], parcels[1:])
    ]
    up_grad = pl.pallas_call(
        sum_kernel,
        grid=(1,),
        out_shape=struct((1, rank, features), f32),
        in_specs=[whole((far_n * near_n, rank, features))],
        out_specs=whole((1, rank, features)),
        compiler_params=params(),
        name="total",
    )(far_parts)

    group = 2 * rank
    projected, gradient = pl.pallas_call(
        functools.partial(finish_kernel, parts),
        grid=(block // features,),
        out_shape=(struct((block, features), bf16), struct((block, width), bf16)),
        in_specs=[
            SMEM,
            SMEM,
            pl.BlockSpec((features, width), lambda i: (i, 0)),
            pl.BlockSpec(own.shape, lambda i: (0, 0)),
        ]
        + [pl.BlockSpec((features, features), lambda i: (i, 0))] * parts
        + [pl.BlockSpec((group, features), lambda i: (block // group + i, 0))] * parts,
        out_specs=(
            pl.BlockSpec((features, features), lambda i: (i, 0)),
            pl.BlockSpec((features, width), lambda i: (i, 0)),
        ),
        compiler_params=params(52),
        cost_estimate=cost(2 * block * width * rank, 5 << 20),
        name="finish",
    )(place, lengths, base, item, *parcels, *parcels)
    return projected, gradient, up_grad


def solution(mesh):
    replicas, parts = mesh.devices.shape
    cores, xlo, near = 2, 2, 4
    sizes = (xlo, replicas // (xlo * near * cores), near, cores)
    fine = Mesh(mesh.devices.reshape(sizes + (parts,)), REP + ("tp",))
    return jax.shard_map(
        functools.partial(on_device, sizes, parts),
        mesh=fine,
        in_specs=(
            P(REP + ("tp",), None),
            P("tp", None),
            P(REP, "tp", None),
            P(REP, None, "tp"),
            P(REP, "tp"),
            P(),
            P(),
        ),
        out_specs=(P(REP, "tp"), P(REP, "tp"), P(REP, None, "tp")),
        check_vma=False,
    )
```

```python
import functools

import jax
import jax.numpy as jnp
from jax import lax
from jax.experimental import pallas as pl
from jax.experimental.pallas import tpu as pltpu
from jax.sharding import Mesh
from jax.sharding import PartitionSpec as P

adapter_scale = 2.0
VMEM = pl.BlockSpec(memory_space=pltpu.VMEM)
SMEM = pl.BlockSpec(memory_space=pltpu.SMEM)
ANY = pl.BlockSpec(memory_space=pl.ANY)
HBM = pl.BlockSpec(memory_space=pltpu.HBM)
REP = ("xlo", "far", "near", "core")


def params(mib=8):
    return pltpu.CompilerParams(vmem_limit_bytes=mib * 1024 * 1024)


def cost(flops, moved):
    return pl.CostEstimate(flops=flops, bytes_accessed=moved, transcendentals=0)


def struct(shape, dtype):
    return jax.ShapeDtypeStruct(shape, dtype)


def whole(shape):
    return pl.BlockSpec(shape, lambda i: (0,) * len(shape))


def dot(a, b, ca, cb):
    return lax.dot_general(
        a, b, (((ca,), (cb,)), ((), ())), preferred_element_type=jnp.float32
    )


def split_place(index, sizes):
    xlo_n, far_n, near_n, core_n = sizes
    core = lax.rem(index, core_n)
    index = lax.div(index, core_n)
    near = lax.rem(index, near_n)
    index = lax.div(index, near_n)
    return lax.div(index, far_n), lax.rem(index, far_n), near, core


def slab_kernel(parts, tokens_ref, upstream_ref, out_ref, slices_ref, fold_ref, sems):
    rows, features = tokens_ref.shape[0], upstream_ref.shape[1]
    width = tokens_ref.shape[1] // parts
    folds = [
        pltpu.make_async_copy(
            upstream_ref.at[pl.ds(g * rows, rows), :],
            fold_ref.at[:, pl.ds(g * features, features)],
            sems.at[1, g],
        )
        for g in range(parts)
    ]
    slices = [
        pltpu.make_async_copy(
            tokens_ref.at[:, pl.ds(s * width, width)], slices_ref.at[s], sems.at[0, s]
        )
        for s in range(parts)
    ]
    for copy in folds + slices:
        copy.start()
    sends = []
    for copy in folds:
        copy.wait()
    for s in range(parts):
        sends.append(
            pltpu.make_async_copy(fold_ref, out_ref.at[s, pl.ds(rows, rows), :], sems.at[2, s])
        )
        sends[-1].start()
    for s in range(parts):
        slices[s].wait()
        sends.append(
            pltpu.make_async_copy(
                slices_ref.at[s], out_ref.at[s, pl.ds(0, rows), :], sems.at[3, s]
            )
        )
        sends[-1].start()
    for copy in sends:
        copy.wait()


def table_kernel(sizes, place_ref, tenants_ref, held_ref, other_ref, out_ref, sems):
    xlo_n, far_n, near_n, core_n = sizes
    _, far, _, core = split_place(place_ref[0], sizes)
    for xlo in range(xlo_n):
        for near in range(near_n):
            block = ((xlo * far_n + far) * near_n + near) * core_n + core
            _, source_far, _, source_core = split_place(tenants_ref[block], sizes)
            slot = xlo * near_n + near

            @pl.when(source_core == core)
            def _():
                pltpu.make_async_copy(
                    held_ref.at[source_far], out_ref.at[slot], sems.at[slot]
                ).start()

            @pl.when(source_core != core)
            def _():
                pltpu.make_async_copy(
                    other_ref.at[source_far], out_ref.at[slot], sems.at[slot]
                ).start()

    for slot in range(xlo_n * near_n):
        pltpu.make_async_copy(held_ref.at[0], out_ref.at[slot], sems.at[slot]).wait()


def unfold(slabs_ref, features):
    sources, _, lanes = slabs_ref.shape
    return jnp.concatenate(
        [
            jnp.concatenate(
                [slabs_ref[s, :, at : at + features] for s in range(sources)], axis=1
            )
            for at in range(0, lanes, features)
        ],
        axis=0,
    )


def value_kernel(partners, columns_ref, weight_ref, *refs):
    outs, mark_ref, held_ref = refs[:-2], refs[-2], refs[-1]
    mark_ref[...] = jnp.zeros_like(mark_ref)
    sources, rows, width = columns_ref.shape
    columns = columns_ref[...].reshape(sources * rows, width)
    held_ref[...] = dot(columns, weight_ref[...], 1, 0).astype(jnp.bfloat16)
    me, features = lax.axis_index("tp"), outs[0].shape[1]
    for k, out_ref in zip(partners, outs):
        at = pl.multiple_of(jnp.bitwise_xor(me, k) * features, features)
        out_ref[...] = held_ref[:, pl.ds(at, features)]


def base_kernel(upstream_ref, weight_ref, out_ref, mark_ref):
    mark_ref[...] = jnp.zeros_like(mark_ref)
    features = weight_ref.shape[1] // upstream_ref.shape[0]
    out_ref[...] = dot(unfold(upstream_ref, features), weight_ref[...], 1, 1)


def low_kernel(
    sizes,
    parts,
    place_ref,
    tenants_ref,
    lengths_ref,
    offered_ref,
    arrived_ref,
    upstream_ref,
    *refs,
):
    outs, share_ref, item_ref, sem = refs[-3 - parts : -3], *refs[-3:]
    place = place_ref[0]
    xlo, _, near, _ = split_place(tenants_ref[place], sizes)
    copy = pltpu.make_async_copy(offered_ref.at[xlo * sizes[2] + near], item_ref, sem)
    copy.start()
    copy.wait()
    sources, rows, width = arrived_ref.shape[0], arrived_ref.shape[1] // 2, arrived_ref.shape[2]
    columns = arrived_ref[:, :rows, :].reshape(sources * rows, width)
    low = dot(item_ref[:, :width], columns, 1, 1)
    back = dot(item_ref[:, width:], upstream_ref[...], 1, 1)
    both = jnp.concatenate([low, back], axis=0).astype(jnp.bfloat16)
    ranks, lanes = both.shape[0], upstream_ref.shape[1]
    for out_ref in outs:
        for g in range(both.shape[1] // lanes):
            out_ref[g * ranks : (g + 1) * ranks, :] = both[:, g * lanes : (g + 1) * lanes]
    live = lax.broadcasted_iota(jnp.int32, low.shape, 1) < lengths_ref[place]
    low = jnp.where(live, adapter_scale * low, 0.0).astype(jnp.bfloat16)
    share = dot(low, unfold(arrived_ref.at[:, rows:, :], lanes), 1, 0)
    for slot in range(share_ref.shape[0]):
        s = slot % parts
        share_ref[slot] = share[:, s * lanes : (s + 1) * lanes].astype(share_ref.dtype)


def route_kernel(sizes, parts, place_ref, tenants_ref, shares_ref, *refs):
    out_ref = refs[-1]
    xlo_n, far_n, near_n, core_n = sizes
    my_xlo, far, near, my_core = split_place(place_ref[0], sizes)
    sums, slots, mine = [], [], []
    for xlo in range(xlo_n):
        for core in range(core_n):
            block = ((xlo * far_n + far) * near_n + near) * core_n + core
            to_xlo, to_far, to_near, to_core = split_place(tenants_ref[block], sizes)
            first = (xlo * core_n + core) * parts
            total = shares_ref[first].astype(jnp.float32)
            for s in range(1, parts):
                total = total + shares_ref[first + s].astype(jnp.float32)
            sums.append(total)
            slots.append(to_far * near_n + to_near)
            mine.append((to_xlo == my_xlo) & (to_core == my_core))
    out_ref[...] = jnp.zeros_like(out_ref)
    for slot, wanted in zip(slots, mine):
        total = jnp.zeros_like(sums[0])
        for other, other_slot, other_wanted in zip(sums, slots, mine):
            total = total + jnp.where(other_wanted & (other_slot == slot), other, 0.0)

        @pl.when(wanted)
        def _():
            out_ref[slot] = total.astype(out_ref.dtype)


def sum_kernel(parts_ref, out_ref):
    total = parts_ref[0].astype(jnp.float32)
    for s in range(1, parts_ref.shape[0]):
        total = total + parts_ref[s].astype(jnp.float32)
    out_ref[0] = total


def presum_kernel(*refs):
    total = refs[0][...].astype(jnp.float32)
    for ref in refs[1:-1]:
        total = total + ref[...].astype(jnp.float32)
    refs[-1][...] = total


def finish_kernel(parts, place_ref, lengths_ref, base_ref, item_ref, *refs):
    values, ranks = refs[:parts], refs[parts : 2 * parts]
    projected_ref, gradient_ref = refs[2 * parts :]
    total = ranks[0][...].astype(jnp.float32)
    for ref in ranks[1:]:
        total = total + ref[...].astype(jnp.float32)
    total = total.astype(jnp.bfloat16).astype(jnp.float32)
    token = lax.broadcasted_iota(jnp.int32, total.shape, 1) + pl.program_id(0) * total.shape[1]
    live = token < lengths_ref[place_ref[0]]
    both = jnp.where(live, adapter_scale * total, 0.0).astype(jnp.bfloat16)
    rank, width = item_ref.shape[0], gradient_ref.shape[1]
    term = dot(both[rank:], item_ref[:, :width], 0, 0)
    gradient_ref[...] = (base_ref[...] + term).astype(jnp.bfloat16)
    value = values[0][...].astype(jnp.float32)
    for ref in values[1:]:
        value = value + ref[...].astype(jnp.float32)
    term = dot(both[:rank], item_ref[:, width:], 0, 0)
    projected_ref[...] = (value + term).astype(jnp.bfloat16)


def on_device(
    sizes, parts, tokens, base_weight, adapter_down, adapter_up, upstream, tenants, lengths
):
    bf16, f32 = jnp.bfloat16, jnp.float32
    xlo_n, far_n, near_n, core_n = sizes
    place = lax.axis_index(REP).astype(jnp.int32).reshape(1)
    rows, full_width = tokens.shape
    width = full_width // parts
    block, features = upstream.shape
    rank = adapter_up.shape[1]
    values = base_weight.shape[1]
    row_step, base_step = 128, 256
    mark = struct((8, 128), f32)
    rank_rows = 2 * rank * block // features
    parcel = struct((block + rank_rows, features), bf16)
    column = xlo_n * core_n * parts
    partners = [0] + sorted(
        range(1, parts), key=lambda k: -(2 * (k % 2) + (0, 1, 2, 1)[k // 2 % 4])
    )
    slabs = pl.pallas_call(
        functools.partial(slab_kernel, parts),
        out_shape=struct((parts, 2 * rows, width), bf16),
        in_specs=[HBM, HBM],
        out_specs=HBM,
        scratch_shapes=[
            pltpu.VMEM((parts, rows, width), bf16),
            pltpu.VMEM((rows, width), bf16),
            pltpu.SemaphoreType.DMA((4, parts)),
        ],
        compiler_params=params(60),
        name="slab",
    )(tokens, upstream)
    arrived = lax.all_to_all(slabs, "tp", 0, 0, tiled=True)

    own = jnp.concatenate([adapter_down[0].T, adapter_up[0]], axis=1)
    held = lax.all_gather(own, "far", axis=0, tiled=False)
    other = lax.ppermute(held, "core", [(c, (c + 1) % core_n) for c in range(core_n)])

    *parcels, value_mark = pl.pallas_call(
        functools.partial(value_kernel, partners),
        grid=(block // row_step,),
        out_shape=[parcel] * parts + [mark],
        in_specs=[
            pl.BlockSpec((row_step // rows, rows, width), lambda i: (i, 0, 0)),
            pl.BlockSpec((width, values), lambda i: (0, 0)),
        ],
        out_specs=[pl.BlockSpec((row_step, features), lambda i: (i, 0))] * parts
        + [whole(mark.shape)],
        scratch_shapes=[pltpu.VMEM((row_step, values), bf16)],
        compiler_params=params(12),
        cost_estimate=cost(2 * block * width * values, 4 << 20),
        name="value",
    )(arrived, base_weight)

    base, base_mark = pl.pallas_call(
        base_kernel,
        grid=(block // base_step,),
        out_shape=(struct((block, width), f32), mark),
        in_specs=[
            pl.BlockSpec(
                (parts, rows, base_step // rows * features), lambda i: (0, 1, i)
            ),
            pl.BlockSpec((width, values), lambda i: (0, 0)),
        ],
        out_specs=(pl.BlockSpec((base_step, width), lambda i: (i, 0)), whole(mark.shape)),
        compiler_params=params(16),
        cost_estimate=cost(2 * block * width * values, 6 << 20),
        name="base",
    )(arrived, base_weight)

    table = pl.pallas_call(
        functools.partial(table_kernel, sizes),
        out_shape=struct((xlo_n * near_n,) + own.shape, bf16),
        in_specs=[SMEM, SMEM, ANY, ANY],
        out_specs=ANY,
        scratch_shapes=[pltpu.SemaphoreType.DMA((xlo_n * near_n,))],
        compiler_params=params(),
        name="table",
    )(place, tenants, held, other)
    offered = lax.all_to_all(table, ("xlo", "near"), 0, 0, tiled=True)

    *parcels, shares, item = pl.pallas_call(
        functools.partial(low_kernel, sizes, parts),
        grid=(1,),
        out_shape=[parcel] * parts
        + [struct((column, rank, features), bf16), struct(own.shape, bf16)],
        in_specs=[SMEM, SMEM, SMEM, ANY, VMEM, VMEM, ANY, ANY] + [ANY] * parts,
        out_specs=[pl.BlockSpec((rank_rows, features), lambda i: (block // rank_rows, 0))]
        * parts
        + [whole((column, rank, features)), whole(own.shape)],
        scratch_shapes=[pltpu.SemaphoreType.DMA],
        input_output_aliases={8 + k: k for k in range(parts)},
        compiler_params=params(12),
        name="low",
    )(place, tenants, lengths, offered, arrived, upstream, value_mark, base_mark, *parcels)
    arrived_shares = lax.all_to_all(shares, ("xlo", "core", "tp"), 0, 0, tiled=True)

    *parcels, routed = pl.pallas_call(
        functools.partial(route_kernel, sizes, parts),
        grid=(1,),
        out_shape=[parcel] * parts + [struct((far_n * near_n, rank, features), bf16)],
        in_specs=[SMEM, SMEM, whole((column, rank, features))] + [ANY] * parts,
        out_specs=[ANY] * parts + [whole((far_n * near_n, rank, features))],
        input_output_aliases={3 + k: k for k in range(parts)},
        compiler_params=params(),
        name="route",
    )(place, tenants, arrived_shares, *parcels)
    far_parts = lax.all_to_all(routed, ("far", "near"), 0, 0, tiled=True)
    parcels = parcels[:1] + [
        lax.ppermute(parcel, "tp", [(d, d ^ k) for d in range(parts)])
        for k, parcel in zip(partners[1:], parcels[1:])
    ]
    up_grad = pl.pallas_call(
        sum_kernel,
        grid=(1,),
        out_shape=struct((1, rank, features), f32),
        in_specs=[whole((far_n * near_n, rank, features))],
        out_specs=whole((1, rank, features)),
        compiler_params=params(),
        name="total",
    )(far_parts)

    group = 2 * rank
    ready = parcels[:-2]
    presum = pl.pallas_call(
        presum_kernel,
        grid=(1,),
        out_shape=struct(parcel.shape, f32),
        in_specs=[whole(parcel.shape)] * len(ready),
        out_specs=whole(parcel.shape),
        compiler_params=params(),
        cost_estimate=cost(len(ready) * parcel.shape[0] * features, 2 << 20),
        name="presum",
    )(*ready)
    parcels = [presum] + parcels[-2:]
    projected, gradient = pl.pallas_call(
        functools.partial(finish_kernel, len(parcels)),
        grid=(block // features,),
        out_shape=(struct((block, features), bf16), struct((block, width), bf16)),
        in_specs=[
            SMEM,
            SMEM,
            pl.BlockSpec((features, width), lambda i: (i, 0)),
            pl.BlockSpec(own.shape, lambda i: (0, 0)),
        ]
        + [pl.BlockSpec((features, features), lambda i: (i, 0))] * len(parcels)
        + [pl.BlockSpec((group, features), lambda i: (block // group + i, 0))] * len(parcels),
        out_specs=(
            pl.BlockSpec((features, features), lambda i: (i, 0)),
            pl.BlockSpec((features, width), lambda i: (i, 0)),
        ),
        compiler_params=params(52),
        cost_estimate=cost(2 * block * width * rank, 5 << 20),
        name="finish",
    )(place, lengths, base, item, *parcels, *parcels)
    return projected, gradient, up_grad


def solution(mesh):
    replicas, parts = mesh.devices.shape
    cores, xlo, near = 2, 2, 4
    sizes = (xlo, replicas // (xlo * near * cores), near, cores)
    fine = Mesh(mesh.devices.reshape(sizes + (parts,)), REP + ("tp",))
    return jax.shard_map(
        functools.partial(on_device, sizes, parts),
        mesh=fine,
        in_specs=(
            P(REP + ("tp",), None),
            P("tp", None),
            P(REP, "tp", None),
            P(REP, None, "tp"),
            P(REP, "tp"),
            P(),
            P(),
        ),
        out_specs=(P(REP, "tp"), P(REP, "tp"), P(REP, None, "tp")),
        check_vma=False,
    )
```
